128 devices in a mesh: section: 4 (over z), tp: 32 (over x, y, core).
Axes of the slice: x: 4, y: 4, z: 4, core: 2. Of those that a mesh axis runs over, the one named last changes fastest.
Arguments:
- entering: bfloat16 [2, 88, 16384], P(None, None, 'tp'), may hold values from -6 to 6
- norm_gain: bfloat16 [4, 16384], P('section', 'tp'), may hold values from 0.099609375 to 1.8984375
- query_weight: bfloat16 [4, 16384, 8192], P(None, ('section', 'tp')), may hold values from -0.046875 to 0.046875
- key_matrix: bfloat16 [4, 16384, 512], P(None, ('section', 'tp')), may hold values from -0.046875 to 0.046875
- value_matrix: bfloat16 [4, 16384, 512], P(None, ('section', 'tp')), may hold values from -0.046875 to 0.046875
- output_weight: bfloat16 [4, 8192, 16384], P(None, ('section', 'tp')), may hold values from -0.0625 to 0.0625
Outputs:
- section_outputs: bfloat16 [4, 2, 88, 16384], P('section', None, None, 'tp')
The draws below stay inside these ranges and needn't reach their ends.
All inputs are finite; a program needn't handle non-finite values.
Results may differ from the reference program's by a relative error of at most 0.017.
Values may be sent and summed in bfloat16 or wider, within the bound.
No kernel may reach another device: no remote copies, remote signals or barrier semaphores. Data moves between devices by JAX's collectives and lax.ppermute only.
A program may use at most 128 MiB of HBM per device.

```python
import math
import jax
import jax.numpy as jnp
from jax import lax

MODEL_WIDTH = 16384
QUERY_HEAD_COUNT = 64
KEY_VALUE_HEADS = 4
HEAD_SIZE = 128
SEQ = 88
M = 2
LAYER_TOTAL = 4


def levels(rng, shape, cuts, smallest, largest):
    gain = 1.0
    for axis_at, shards_of in cuts:
        steps = jax.random.uniform(jax.random.fold_in(jax.random.fold_in(rng, 6), axis_at), (shards_of,), jnp.float32, smallest / len(cuts), largest / len(cuts))
        gain = gain * jnp.repeat(jnp.exp(steps), shape[axis_at] // shards_of).reshape((-1,) + (1,) * (len(shape) - 1 - axis_at))
    return gain


def scatter_about(rng, shape, width, limit, cuts=(), held_as=jnp.bfloat16):
    drawn = width * jax.random.normal(rng, shape, jnp.float32)
    if cuts:
        drawn = drawn * levels(rng, shape, cuts, -0.22, 0.18)
    return jnp.clip(drawn, -limit, limit).astype(held_as)


def setup_inputs(seed: int = 0) -> dict:
    key_of = jax.random.split(jax.random.key(seed), 7)
    entering = scatter_about(key_of[0], (M, SEQ, MODEL_WIDTH), 1.0, 6.0, ((2, 32),))
    norm_gain = jnp.clip(1.0 + 0.18 * jax.random.normal(key_of[1], (LAYER_TOTAL, MODEL_WIDTH), jnp.float32), 0.099609375, 1.8984375).astype(jnp.bfloat16)
    query_weight = scatter_about(key_of[2], (LAYER_TOTAL, MODEL_WIDTH, QUERY_HEAD_COUNT * HEAD_SIZE), MODEL_WIDTH ** -0.5, 0.046875, ((1, 128),))
    key_matrix = scatter_about(key_of[3], (LAYER_TOTAL, MODEL_WIDTH, KEY_VALUE_HEADS * HEAD_SIZE), MODEL_WIDTH ** -0.5, 0.046875, ((1, 128),))
    value_matrix = scatter_about(key_of[4], (LAYER_TOTAL, MODEL_WIDTH, KEY_VALUE_HEADS * HEAD_SIZE), MODEL_WIDTH ** -0.5, 0.046875, ((1, 128),))
    output_weight = scatter_about(key_of[5], (LAYER_TOTAL, QUERY_HEAD_COUNT * HEAD_SIZE, MODEL_WIDTH), (QUERY_HEAD_COUNT * HEAD_SIZE) ** -0.5, 0.0625, ((1, 128),))
    return dict(entering=entering, norm_gain=norm_gain, query_weight=query_weight, key_matrix=key_matrix, value_matrix=value_matrix, output_weight=output_weight)


def attend_layer(hidden, gain_row, query_w, key_w, value_w, output_w):
    local_token_count = hidden.shape[0]
    query_group_width = QUERY_HEAD_COUNT // KEY_VALUE_HEADS
    widened = hidden.astype(jnp.float32)
    normed = (widened * lax.rsqrt(lax.optimization_barrier(jnp.mean(widened * widened, axis=-1, keepdims=True)) + 1e-05) * gain_row.astype(jnp.float32)).astype(jnp.bfloat16)
    query_rows = jnp.dot(normed, query_w, preferred_element_type=jnp.float32).astype(jnp.bfloat16)
    key_row_block = jnp.dot(normed, key_w, preferred_element_type=jnp.float32).astype(jnp.bfloat16)
    value_row_block = jnp.dot(normed, value_w, preferred_element_type=jnp.float32).astype(jnp.bfloat16)
    query_float = query_rows.astype(jnp.float32).reshape(local_token_count, KEY_VALUE_HEADS, query_group_width, HEAD_SIZE)
    key_float = key_row_block.astype(jnp.float32).reshape(local_token_count, KEY_VALUE_HEADS, HEAD_SIZE)
    value_float = value_row_block.astype(jnp.float32).reshape(local_token_count, KEY_VALUE_HEADS, HEAD_SIZE)
    scale_factor = 1.0 / math.sqrt(HEAD_SIZE)
    scores = jnp.einsum('sgjd,tgd->gjst', query_float, key_float) * scale_factor
    causal = jnp.arange(local_token_count)[:, None] >= jnp.arange(local_token_count)[None, :]
    weights = jnp.where(causal, jnp.exp(scores), 0.0)
    shares = (weights / lax.optimization_barrier(jnp.sum(weights, axis=-1, keepdims=True))).astype(jnp.bfloat16)
    head_mixed = jnp.einsum('gjst,tgd->sgjd', shares.astype(jnp.float32), value_float)
    head_mixed = head_mixed.astype(jnp.bfloat16).reshape(local_token_count, QUERY_HEAD_COUNT * HEAD_SIZE)
    return (widened + jnp.dot(head_mixed, output_w, preferred_element_type=jnp.float32)).astype(jnp.bfloat16)

def reference(entering, norm_gain, query_weight, key_matrix, value_matrix, output_weight):
    layer_count = query_weight.shape[0]
    current = [entering[batch_index] for batch_index in range(entering.shape[0])]
    collected = []
    for layer_index in range(layer_count):
        current = [attend_layer(item, norm_gain[layer_index], query_weight[layer_index], key_matrix[layer_index], value_matrix[layer_index], output_weight[layer_index]) for item in current]
        collected.append(jnp.stack(current))
    return jnp.stack(collected)
```

```python
import functools
import math

import jax
import jax.numpy as jnp
from jax import lax
from jax.experimental import pallas as pl
from jax.experimental.pallas import tpu as pltpu
from jax.sharding import Mesh, PartitionSpec as P


CHIPS = ("z", "x", "y")
PLANE = ("x", "y")
ALL = ("z", "x", "y", "c")
N = 64
HEAD = 128
SEQ = 88
COLS = 256
WIDTH = 16384
ROWS = 112
STEPS = 8
VMEM_LIMIT = 48 * 1024 * 1024
f32 = jnp.float32
bf16 = jnp.bfloat16


def dot(a, b, contract=((1,), (0,))):
    return lax.dot_general(a, b, (contract, ((), ())), preferred_element_type=f32)


def eye_mask():
    rows = lax.broadcasted_iota(jnp.int32, (SEQ, 128), 0)
    lanes = lax.broadcasted_iota(jnp.int32, (SEQ, 128), 1)
    return rows == lanes, lanes <= rows


def prepare(core_ref, x, gain_ref, xg_ref, xgp_ref, ss_ref):
    wide = x.astype(f32)
    eye, _ = eye_mask()
    column = jnp.sum(wide * wide, axis=1, keepdims=True)
    row = jnp.sum(jnp.where(eye, column, 0.0), axis=0, keepdims=True)
    high = row.astype(bf16).astype(f32)
    low = row - high
    which = lax.broadcasted_iota(jnp.int32, (8, 128), 0)
    ss_ref[...] = jnp.where(which == 0, high, jnp.where(which == 1, low, 0.0))
    scaled = wide * gain_ref[...].astype(f32)
    turned = jnp.concatenate([scaled[:, 128:], scaled[:, :128]], axis=1)
    scaled = jnp.where(core_ref[0] == 1, turned, scaled)
    xg_ref[...] = scaled.astype(bf16)
    xgp_ref[...] = jnp.concatenate([scaled, jnp.zeros((128 - SEQ, COLS), f32)], axis=0).astype(bf16)


def project_kernel(lead, core_ref, *refs):
    if lead:
        recv_ref, *refs = refs
    x_ref, gain_ref, wq0, wq1, wk0, wk1, wv0, wv1, *refs = refs
    if lead:
        out_ref, new_ref, acc, xg_ref, xgp_ref, ss_ref, kv_ref = refs
    else:
        out_ref, xg_ref, xgp_ref, ss_ref, kv_ref = refs
    step = pl.program_id(0)
    if lead:

        @pl.when(step == 0)
        def _():
            acc[...] = x_ref[...].astype(f32)

        @pl.when(step < lead)
        def _():
            acc[...] += jnp.sum(recv_ref[...].astype(f32), axis=0)

        @pl.when(step == lead - 1)
        def _():
            new = acc[...].astype(bf16)
            new_ref[...] = new
            prepare(core_ref, new, gain_ref, xg_ref, xgp_ref, ss_ref)
    else:

        @pl.when(step == 0)
        def _():
            prepare(core_ref, x_ref[...], gain_ref, xg_ref, xgp_ref, ss_ref)

    @pl.when(step >= lead)
    def _():
        turn = lax.rem(step - lead, 2)

        @pl.when(turn == 0)
        def _():
            kv_ref[...] = dot(xgp_ref[...], jnp.concatenate([wk0[0], wk1[0]], axis=0)).T

        @pl.when(turn == 1)
        def _():
            kv_ref[...] = dot(xgp_ref[...], jnp.concatenate([wv0[0], wv1[0]], axis=0)).T

        q = dot(xg_ref[...], jnp.concatenate([wq0[0], wq1[0]], axis=0))
        for h in range(8):
            out_ref[h] = jnp.concatenate(
                [kv_ref[16 * h : 16 * h + 16], ss_ref[...], q[:, HEAD * h : HEAD * h + HEAD]], axis=0
            ).astype(bf16)


def project(layer, core, received, x, gain, weights):
    lead = 0 if received is None else STEPS
    at = lambda s: jnp.maximum(s - lead, 0)
    whole = lambda *shape: pl.BlockSpec(shape, lambda s: (0,) * len(shape))
    specs = [pl.BlockSpec(memory_space=pltpu.SMEM)]
    args = [core]
    if lead:
        specs.append(pl.BlockSpec((N // STEPS, SEQ, COLS), lambda s: (jnp.minimum(s, lead - 1), 0, 0)))
        args.append(received)
    specs += [whole(SEQ, COLS), whole(1, COLS)]
    args += [x, gain]
    own, other = weights
    for name, width in (("q", 1024), ("k", 128), ("v", 128)):
        for array in (own[name], other[name]):
            index = layer if array.shape[0] > 1 else 0
            if name == "q":
                index_map = lambda s, index=index: (index, 0, at(s))
            else:
                index_map = lambda s, index=index: (index, 0, at(s) // 2)
            specs.append(pl.BlockSpec((1, 128, width), index_map))
            args.append(array)
    outs = [jax.ShapeDtypeStruct((N, ROWS, 128), bf16)]
    out_specs = [pl.BlockSpec((8, ROWS, 128), lambda s: (at(s), 0, 0))]
    scratch = [
        pltpu.VMEM((SEQ, COLS), bf16),
        pltpu.VMEM((128, COLS), bf16),
        pltpu.VMEM((8, 128), f32),
        pltpu.VMEM((128, 128), f32),
    ]
    if lead:
        outs.append(jax.ShapeDtypeStruct((SEQ, COLS), bf16))
        out_specs.append(whole(SEQ, COLS))
        scratch = [pltpu.VMEM((SEQ, COLS), f32)] + scratch
    result = pl.pallas_call(
        functools.partial(project_kernel, lead),
        grid=(lead + STEPS,),
        in_specs=specs,
        out_specs=out_specs,
        out_shape=outs,
        scratch_shapes=scratch,
        compiler_params=pltpu.CompilerParams(vmem_limit_bytes=VMEM_LIMIT),
        cost_estimate=pl.CostEstimate(
            flops=2 * SEQ * COLS * 9216, bytes_accessed=10_000_000, transcendentals=0
        ),
        name="project",
    )(*args)
    return result if lead else (result[0], x)


def gather_kernel(recv_ref, q_ref, kv_ref, acc):
    step = pl.program_id(0)

    @pl.when(step == 0)
    def _():
        acc[...] = jnp.zeros_like(acc)

    acc[...] += jnp.sum(recv_ref[...].astype(f32), axis=0)

    @pl.when(step == STEPS - 1)
    def _():
        total = acc[16:17] + acc[17:18]
        row = lax.rsqrt(total * (1.0 / WIDTH) + 1e-05)
        eye, _ = eye_mask()
        column = jnp.sum(jnp.where(eye, row, 0.0), axis=1, keepdims=True)
        q_ref[...] = (acc[24:] * column).astype(bf16)
        kv_ref[...] = jnp.broadcast_to((acc[:16] * row)[None], kv_ref.shape).astype(bf16)


def gather(received):
    return pl.pallas_call(
        gather_kernel,
        grid=(STEPS,),
        in_specs=[pl.BlockSpec((N // STEPS, ROWS, 128), lambda s: (s, 0, 0))],
        out_specs=[
            pl.BlockSpec((SEQ, HEAD), lambda s: (0, 0)),
            pl.BlockSpec((16, 16, 128), lambda s: (0, 0, 0)),
        ],
        out_shape=[
            jax.ShapeDtypeStruct((SEQ, HEAD), bf16),
            jax.ShapeDtypeStruct((16, 16, 128), bf16),
        ],
        scratch_shapes=[pltpu.VMEM((ROWS, 128), f32)],
        compiler_params=pltpu.CompilerParams(vmem_limit_bytes=VMEM_LIMIT),
        cost_estimate=pl.CostEstimate(flops=2_000_000, bytes_accessed=2_000_000, transcendentals=0),
        name="collect",
    )(received)


def attend_kernel(core_ref, q_ref, kv_ref, wo0, wo1, out_ref, mixed_ref):
    step = pl.program_id(0)

    @pl.when(step == 0)
    def _():
        kv = kv_ref[...].reshape(256, 128)
        _, causal = eye_mask()
        scores = dot(q_ref[...], kv[:128]) * (1.0 / math.sqrt(HEAD))
        weights = jnp.where(causal, jnp.exp(scores), 0.0)
        shares = (weights / jnp.sum(weights, axis=1, keepdims=True)).astype(bf16)
        mixed = dot(shares, kv[128:], ((1,), (1,)))
        turned = jnp.concatenate([mixed[:, 64:], mixed[:, :64]], axis=1)
        mixed_ref[...] = jnp.where(core_ref[0] == 1, turned, mixed).astype(bf16)

    o = dot(mixed_ref[...], jnp.concatenate([wo0[0], wo1[0]], axis=0))
    for i in range(8):
        out_ref[i] = o[:, COLS * i : COLS * i + COLS].astype(bf16)


def attend(layer, core, q, kv, weights):
    arrays = [w["o"] for w in weights]
    return pl.pallas_call(
        attend_kernel,
        grid=(STEPS,),
        in_specs=[
            pl.BlockSpec(memory_space=pltpu.SMEM),
            pl.BlockSpec((SEQ, HEAD), lambda s: (0, 0)),
            pl.BlockSpec((16, 16, 128), lambda s: (0, 0, 0)),
        ]
        + [
            pl.BlockSpec((1, 64, 2048), lambda s, index=layer if w.shape[0] > 1 else 0: (index, 0, s))
            for w in arrays
        ],
        out_specs=pl.BlockSpec((8, SEQ, COLS), lambda s: (s, 0, 0)),
        out_shape=jax.ShapeDtypeStruct((N, SEQ, COLS), bf16),
        scratch_shapes=[pltpu.VMEM((SEQ, HEAD), bf16)],
        compiler_params=pltpu.CompilerParams(vmem_limit_bytes=VMEM_LIMIT),
        cost_estimate=pl.CostEstimate(
            flops=2 * SEQ * HEAD * WIDTH, bytes_accessed=7_000_000, transcendentals=0
        ),
        name="attend",
    )(core, q, kv, *arrays)


def close_kernel(recv_ref, x_ref, out_ref, acc):
    step = pl.program_id(0)

    @pl.when(step == 0)
    def _():
        acc[...] = x_ref[...].astype(f32)

    acc[...] += jnp.sum(recv_ref[...].astype(f32), axis=0)

    @pl.when(step == STEPS - 1)
    def _():
        out_ref[...] = acc[...].astype(bf16)


def close(received, x):
    return pl.pallas_call(
        close_kernel,
        grid=(STEPS,),
        in_specs=[
            pl.BlockSpec((N // STEPS, SEQ, COLS), lambda s: (s, 0, 0)),
            pl.BlockSpec((SEQ, COLS), lambda s: (0, 0)),
        ],
        out_specs=pl.BlockSpec((SEQ, COLS), lambda s: (0, 0)),
        out_shape=jax.ShapeDtypeStruct((SEQ, COLS), bf16),
        scratch_shapes=[pltpu.VMEM((SEQ, COLS), f32)],
        compiler_params=pltpu.CompilerParams(vmem_limit_bytes=VMEM_LIMIT),
        cost_estimate=pl.CostEstimate(flops=3_000_000, bytes_accessed=3_000_000, transcendentals=0),
        name="close",
    )(received, x)


def exchange(value, axes):
    return lax.all_to_all(value, axes, 0, 0, tiled=True)


def swap(value):
    return lax.ppermute(value, "c", [(0, 1), (1, 0)])


def body(entering, norm_gain, query_weight, key_matrix, value_matrix, output_weight):
    plane = lax.axis_index("z")
    core = lax.axis_index("c")
    half = lax.rem(lax.axis_index("y"), 2)
    slot = 2 * core + half
    core_array = core.astype(jnp.int32).reshape(1)

    x = None
    for m in range(2):
        for h in range(2):
            pairs = [(32 * (i // 16) + i // 2, 2 * i + m) for i in range(h, N, 2)]
            piece = lax.ppermute(entering[m, :, COLS * h : COLS * h + COLS], ALL, pairs)
            x = piece if x is None else x + piece
    rounds = []
    for k in range(4):
        pairs = [
            (32 * ((2 * c + i % 2 + k) % 4) + i // 2, 2 * i + c) for i in range(N) for c in range(2)
        ]
        piece = lax.dynamic_slice_in_dim(norm_gain, lax.rem(plane + 4 - k, 2) * COLS, COLS, 1)
        rounds.append(lax.ppermute(piece, ALL, pairs))
    rounds = jnp.stack(rounds)
    gains = [
        lax.dynamic_index_in_dim(rounds, lax.rem(layer - slot + 4, 4), 0, keepdims=False)
        for layer in range(4)
    ]

    own = dict(q=query_weight, k=key_matrix, v=value_matrix, o=output_weight)
    other_k = swap(key_matrix)
    other_v = swap(value_matrix)
    others = [
        dict(
            q=swap(query_weight[layer : layer + 1]),
            k=other_k,
            v=other_v,
            o=swap(output_weight[layer : layer + 1]),
        )
        for layer in range(4)
    ]

    received = None
    states = []
    for layer in range(4):
        weights = (own, others[layer])
        partial, x = project(layer, core_array, received, x, gains[layer], weights)
        if layer:
            states.append(x)
        q, kv = gather(exchange(partial, CHIPS))
        received = exchange(attend(layer, core_array, q, exchange(kv, PLANE), weights), CHIPS)
    states.append(close(received, x))

    states = jnp.stack(states)
    rounds = []
    for k in range(4):
        pairs = [
            (2 * i + c, 32 * ((2 * c + i % 2 + k) % 4) + i // 2) for i in range(N) for c in range(2)
        ]
        piece = lax.dynamic_index_in_dim(states, lax.rem(slot + k, 4), 0, keepdims=False)
        rounds.append(lax.ppermute(piece, ALL, pairs))
    rounds = jnp.stack(rounds)
    pieces = [
        lax.dynamic_index_in_dim(rounds, lax.rem(plane - s + 4, 4), 0, keepdims=False) for s in range(4)
    ]
    return jnp.stack(
        [jnp.concatenate(pieces[:2], axis=1), jnp.concatenate(pieces[2:], axis=1)]
    )[None]


def solution(mesh):
    fine = Mesh(mesh.devices.reshape(4, 4, 4, 2), ALL)
    tp = ("x", "y", "c")
    rows = P(None, ALL, None)
    return jax.shard_map(
        body,
        mesh=fine,
        in_specs=(P(None, None, tp), P("z", tp), rows, rows, rows, rows),
        out_specs=P("z", None, None, tp),
        check_vma=False,
    )
```

```python
import functools
import math

import jax
import jax.numpy as jnp
from jax import lax
from jax.experimental import pallas as pl
from jax.experimental.pallas import tpu as pltpu
from jax.sharding import Mesh, PartitionSpec as P


ALL = ("z", "x", "y", "c")
HEAD = 128
SEQ = 88
COLS = 256
WIDTH = 16384
SLAB = 2304
OCOLS = 4096
ROWS = 352
VMEM_LIMIT = 48 * 1024 * 1024
f32 = jnp.float32
bf16 = jnp.bfloat16
SMEM = pl.BlockSpec(memory_space=pltpu.SMEM)
PARAMS = pltpu.CompilerParams(vmem_limit_bytes=VMEM_LIMIT)


def dot(a, b, contract=((1,), (0,))):
    return lax.dot_general(a, b, (contract, ((), ())), preferred_element_type=f32)


def whole(*shape):
    return pl.BlockSpec(shape, lambda s: (0,) * len(shape))


def cost(flops, size):
    return pl.CostEstimate(flops=flops, bytes_accessed=size, transcendentals=0)


def masks():
    rows = lax.broadcasted_iota(jnp.int32, (SEQ, 128), 0)
    lanes = lax.broadcasted_iota(jnp.int32, (SEQ, 128), 1)
    return rows == lanes, lanes <= rows


def slab_in_kernel(scalars, q_ref, k_ref, v_ref, *outs):
    for k, out in enumerate(outs):
        at = lax.rem(scalars[0] + k, 4)
        out[:, :2048] = q_ref[0, :, pl.ds(pl.multiple_of(at * 2048, 2048), 2048)]
        out[:, 2048:2176] = k_ref[0, :, pl.ds(pl.multiple_of(at * 128, 128), 128)]
        out[:, 2176:] = v_ref[0, :, pl.ds(pl.multiple_of(at * 128, 128), 128)]


def slab_in(layer, scalars, q, k, v):
    return pl.pallas_call(
        slab_in_kernel,
        grid=(4,),
        in_specs=[
            SMEM,
            pl.BlockSpec((1, 32, 8192), lambda s: (layer, s, 0)),
            pl.BlockSpec((1, 32, 512), lambda s: (layer, s, 0)),
            pl.BlockSpec((1, 32, 512), lambda s: (layer, s, 0)),
        ],
        out_specs=[pl.BlockSpec((32, SLAB), lambda s: (s, 0))] * 4,
        out_shape=[jax.ShapeDtypeStruct((128, SLAB), bf16)] * 4,
        compiler_params=PARAMS,
        cost_estimate=cost(0, 4_700_000),
        name="slab_in",
    )(scalars, q, k, v)


def slab_out_kernel(scalars, o_ref, *outs):
    for k, out in enumerate(outs):
        at = lax.rem(scalars[1] + k, 4) * COLS
        for s in range(16):
            out[:, COLS * s : COLS * s + COLS] = o_ref[
                0, :, pl.ds(pl.multiple_of(at + 1024 * s, COLS), COLS)
            ]


def slab_out(layer, scalars, o):
    return pl.pallas_call(
        slab_out_kernel,
        grid=(4,),
        in_specs=[SMEM, pl.BlockSpec((1, 16, WIDTH), lambda s: (layer, s, 0))],
        out_specs=[pl.BlockSpec((16, OCOLS), lambda s: (s, 0))] * 4,
        out_shape=[jax.ShapeDtypeStruct((64, OCOLS), bf16)] * 4,
        compiler_params=PARAMS,
        cost_estimate=cost(0, 4_200_000),
        name="slab_out",
    )(scalars, o)


def project_kernel(layer, scalars, *refs):
    xs, gain_ref, ws, kvs, refs = refs[:4], refs[4], refs[5:13], refs[13:21], refs[21:]
    out_ref, xg_ref, ss_ref, kv_ref = refs
    z, core = scalars[0], scalars[2]

    @pl.when(pl.program_id(0) == 0)
    def _():
        gains = gain_ref[lax.rem(z - layer + 4, 4)]
        at = lax.broadcasted_iota(jnp.int32, (4, COLS), 0)
        total = jnp.zeros((SEQ, 1), f32)
        parts = []
        for k in range(4):
            wide = xs[k][...].astype(f32)
            total += jnp.sum(wide * wide, axis=1, keepdims=True)
            gain = jnp.sum(jnp.where(at == lax.rem(z - k + 4, 4), gains, 0.0), axis=0, keepdims=True)
            scaled = wide * gain
            turned = jnp.concatenate([scaled[:, 128:], scaled[:, :128]], axis=1)
            parts.append(jnp.where(core == 1, turned, scaled))
        scaled = jnp.concatenate(parts, axis=1)
        xg_ref[...] = scaled.astype(bf16)
        padded = jnp.concatenate([scaled, jnp.zeros((128 - SEQ, 1024), f32)], axis=0).astype(bf16)
        eye, _ = masks()
        row = jnp.sum(jnp.where(eye, total, 0.0), axis=0, keepdims=True)
        high = row.astype(bf16).astype(f32)
        which = lax.broadcasted_iota(jnp.int32, (8, 128), 0)
        ss_ref[...] = jnp.where(which == 0, high, jnp.where(which == 1, row - high, 0.0))
        kv = dot(padded, jnp.concatenate([w[...] for w in kvs], axis=0))
        kv_ref[:128] = kv[:, :128].T
        kv_ref[128:] = kv[:, 128:].T

    q = dot(xg_ref[...], jnp.concatenate([w[...] for w in ws], axis=0))
    for h in range(4):
        out_ref[h] = jnp.concatenate(
            [kv_ref[...], ss_ref[...], q[:, HEAD * h : HEAD * h + HEAD]], axis=0
        ).astype(bf16)


def project(layer, scalars, xs, gains, weights):
    return pl.pallas_call(
        functools.partial(project_kernel, layer),
        grid=(4,),
        in_specs=[SMEM]
        + [whole(SEQ, COLS)] * 4
        + [whole(4, 4, COLS)]
        + [pl.BlockSpec((128, 512), lambda s: (0, s))] * 8
        + [pl.BlockSpec((128, 256), lambda s: (0, 8))] * 8,
        out_specs=pl.BlockSpec((4, ROWS, 128), lambda s: (s, 0, 0)),
        out_shape=jax.ShapeDtypeStruct((16, ROWS, 128), bf16),
        scratch_shapes=[
            pltpu.VMEM((SEQ, 1024), bf16),
            pltpu.VMEM((8, 128), f32),
            pltpu.VMEM((256, 128), f32),
        ],
        compiler_params=PARAMS,
        cost_estimate=cost(2 * SEQ * 1024 * SLAB, 6_500_000),
        name="project",
    )(scalars, *xs, gains, *weights, *weights)


def attend_kernel(recv_ref, out_ref, acc):
    step = pl.program_id(0)

    @pl.when(step == 0)
    def _():
        acc[...] = jnp.sum(recv_ref[...].astype(f32), axis=0)

    @pl.when(step > 0)
    def _():
        acc[...] += jnp.sum(recv_ref[...].astype(f32), axis=0)

    @pl.when(step == 3)
    def _():
        total = acc[256:257] + acc[257:258]
        row = lax.rsqrt(total * (1.0 / WIDTH) + 1e-05)
        eye, causal = masks()
        column = jnp.sum(jnp.where(eye, row, 0.0), axis=1, keepdims=True)
        q = (acc[264:] * column).astype(bf16)
        keys = (acc[:128] * row).astype(bf16)
        values = (acc[128:256] * row).astype(bf16)
        scores = dot(q, keys) * (1.0 / math.sqrt(HEAD))
        weights = jnp.where(causal, jnp.exp(scores), 0.0)
        shares = (weights / jnp.sum(weights, axis=1, keepdims=True)).astype(bf16)
        out_ref[...] = dot(shares, values, ((1,), (1,))).astype(bf16)


def attend(received):
    return pl.pallas_call(
        attend_kernel,
        grid=(4,),
        in_specs=[pl.BlockSpec((4, ROWS, 128), lambda s: (s, 0, 0))],
        out_specs=whole(SEQ, HEAD),
        out_shape=jax.ShapeDtypeStruct((SEQ, HEAD), bf16),
        scratch_shapes=[pltpu.VMEM((ROWS, 128), f32)],
        compiler_params=PARAMS,
        cost_estimate=cost(6_000_000, 1_500_000),
        name="attend",
    )(received)


def output_kernel(scalars, *refs):
    mixed, ws, out_ref, mixed_ref = refs[:4], refs[4:12], refs[12], refs[13]

    @pl.when(pl.program_id(0) == 0)
    def _():
        parts = []
        for part in mixed:
            part = part[...].astype(f32)
            turned = jnp.concatenate([part[:, 64:], part[:, :64]], axis=1)
            parts.append(jnp.where(scalars[2] == 1, turned, part))
        mixed_ref[...] = jnp.concatenate(parts, axis=1).astype(bf16)

    o = dot(mixed_ref[...], jnp.concatenate([w[...] for w in ws], axis=0))
    for i in range(4):
        out_ref[i] = o[:, COLS * i : COLS * i + COLS].astype(bf16)


def output(scalars, mixed, weights):
    return pl.pallas_call(
        output_kernel,
        grid=(4,),
        in_specs=[SMEM]
        + [whole(SEQ, HEAD)] * 4
        + [pl.BlockSpec((64, 1024), lambda s: (0, s))] * 8,
        out_specs=pl.BlockSpec((4, SEQ, COLS), lambda s: (s, 0, 0)),
        out_shape=jax.ShapeDtypeStruct((16, SEQ, COLS), bf16),
        scratch_shapes=[pltpu.VMEM((SEQ, 512), bf16)],
        compiler_params=PARAMS,
        cost_estimate=cost(2 * SEQ * 512 * OCOLS, 5_000_000),
        name="output",
    )(scalars, *mixed, *weights)


def close_kernel(recv_ref, x_ref, out_ref):
    out_ref[...] = (x_ref[...].astype(f32) + jnp.sum(recv_ref[...].astype(f32), axis=0)).astype(bf16)


def close(received, x):
    return pl.pallas_call(
        close_kernel,
        grid=(1,),
        in_specs=[whole(16, SEQ, COLS), whole(SEQ, COLS)],
        out_specs=whole(SEQ, COLS),
        out_shape=jax.ShapeDtypeStruct((SEQ, COLS), bf16),
        compiler_params=PARAMS,
        cost_estimate=cost(400_000, 800_000),
        name="close",
    )(received, x)


def exchange(value, axes):
    return lax.all_to_all(value, axes, 0, 0, tiled=True)


def shift(value, axis, by):
    return lax.ppermute(value, axis, [(i, (i + by) % 4) for i in range(4)])


def line(value, axis):
    return [value] + [shift(value, axis, k) for k in range(1, 4)]


def gated(values, gate):
    return lax.optimization_barrier((values, gate))[0]


def relay(slabs, axis):
    pieces = [slabs[0]] + [shift(slabs[k], axis, k) for k in range(1, 4)]
    others = [lax.ppermute(piece, "c", [(0, 1), (1, 0)]) for piece in pieces]
    return [side for pair in zip(pieces, others) for side in pair]


def body(entering, norm_gain, query_weight, key_matrix, value_matrix, output_weight):
    plane, across, along, core = (lax.axis_index(name) for name in ALL)
    slot = 2 * core + lax.rem(along, 2)
    scalars = jnp.stack([plane, along, core]).astype(jnp.int32)

    rounds = []
    for r in range(4):
        pairs = []
        for p in range(4):
            for t in range(32):
                s = (t // 8 - r) % 4
                pairs.append((32 * p + t, 32 * p + 2 * ((2 * t) % 16 + s % 2) + s // 2))
        s = lax.rem(across - r + 4, 4)
        piece = lax.dynamic_slice(entering, (s // 2, 0, lax.rem(s, 2) * COLS), (1, SEQ, COLS))[0]
        gain = lax.dynamic_slice(norm_gain, (0, lax.rem(s, 2) * COLS), (1, COLS))
        piece = jnp.concatenate([piece, jnp.broadcast_to(gain, (8, COLS))], axis=0)
        rounds.append(lax.ppermute(piece, ALL, pairs))
    rounds = jnp.stack(rounds)
    xs = [
        lax.dynamic_index_in_dim(rounds, lax.rem(plane - k - slot + 8, 4), 0, keepdims=False)[:SEQ]
        for k in range(4)
    ]
    gains = jnp.stack([rounds[:, SEQ][lax.rem(p - slot + 4, 4)] for p in range(4)])
    gains = jnp.stack(line(gains, "z")).astype(f32)

    ins = relay(slab_in(0, scalars, query_weight, key_matrix, value_matrix), "z")
    outs = relay(gated(slab_out(0, scalars, output_weight), ins[-2]), "y")
    states = []
    for layer in range(4):
        partial = project(layer, scalars, xs, gains, ins)
        if layer < 3:
            slabs = slab_in(layer + 1, scalars, query_weight, key_matrix, value_matrix)
            ins = relay(gated(slabs, partial), "z")
        mixed = attend(exchange(partial, ("x", "y")))
        partial = output(scalars, line(mixed, "y"), outs)
        if layer < 3:
            outs = relay(gated(slab_out(layer + 1, scalars, output_weight), partial), "y")
        x = close(exchange(partial, ("z", "x")), xs[0])
        states.append(x)
        if layer < 3:
            xs = line(x, "z")

    states = jnp.stack(states)
    rounds = []
    for k in range(4):
        pairs = [
            (2 * i + c, 32 * ((2 * c + i % 2 + k) % 4) + i // 2) for i in range(64) for c in range(2)
        ]
        piece = lax.dynamic_index_in_dim(states, lax.rem(slot + k, 4), 0, keepdims=False)
        rounds.append(lax.ppermute(piece, ALL, pairs))
    rounds = jnp.stack(rounds)
    pieces = [
        lax.dynamic_index_in_dim(rounds, lax.rem(plane - s + 4, 4), 0, keepdims=False) for s in range(4)
    ]
    return jnp.stack(
        [jnp.concatenate(pieces[:2], axis=1), jnp.concatenate(pieces[2:], axis=1)]
    )[None]


def solution(mesh):
    fine = Mesh(mesh.devices.reshape(4, 4, 4, 2), ALL)
    tp = ("x", "y", "c")
    rows = P(None, ALL, None)
    return jax.shard_map(
        body,
        mesh=fine,
        in_specs=(P(None, None, tp), P("z", tp), rows, rows, rows, rows),
        out_specs=P("z", None, None, tp),
        check_vma=False,
    )
```

```python
import functools
import math

import jax
import jax.numpy as jnp
from jax import lax
from jax.experimental import pallas as pl
from jax.experimental.pallas import tpu as pltpu
from jax.sharding import Mesh, PartitionSpec as P


ALL = ("z", "x", "y", "c")
HEAD = 128
SEQ = 88
COLS = 256
WIDTH = 16384
SLAB = 2304
OCOLS = 4096
ROWS = 352
VMEM_LIMIT = 48 * 1024 * 1024
f32 = jnp.float32
bf16 = jnp.bfloat16
SMEM = pl.BlockSpec(memory_space=pltpu.SMEM)
PARAMS = pltpu.CompilerParams(vmem_limit_bytes=VMEM_LIMIT)


def dot(a, b, contract=((1,), (0,))):
    return lax.dot_general(a, b, (contract, ((), ())), preferred_element_type=f32)


def whole(*shape):
    return pl.BlockSpec(shape, lambda s: (0,) * len(shape))


def cost(flops, size):
    return pl.CostEstimate(flops=flops, bytes_accessed=size, transcendentals=0)


def masks():
    rows = lax.broadcasted_iota(jnp.int32, (SEQ, 128), 0)
    lanes = lax.broadcasted_iota(jnp.int32, (SEQ, 128), 1)
    return rows == lanes, lanes <= rows


def slab_in_kernel(scalars, q_ref, k_ref, v_ref, *outs):
    for k, out in enumerate(outs):
        at = lax.rem(scalars[0] + k, 4)
        out[:, :2048] = q_ref[0, :, pl.ds(pl.multiple_of(at * 2048, 2048), 2048)]
        out[:, 2048:2176] = k_ref[0, :, pl.ds(pl.multiple_of(at * 128, 128), 128)]
        out[:, 2176:] = v_ref[0, :, pl.ds(pl.multiple_of(at * 128, 128), 128)]


def slab_in(layer, scalars, q, k, v):
    return pl.pallas_call(
        slab_in_kernel,
        grid=(4,),
        in_specs=[
            SMEM,
            pl.BlockSpec((1, 32, 8192), lambda s: (layer, s, 0)),
            pl.BlockSpec((1, 32, 512), lambda s: (layer, s, 0)),
            pl.BlockSpec((1, 32, 512), lambda s: (layer, s, 0)),
        ],
        out_specs=[pl.BlockSpec((32, SLAB), lambda s: (s, 0))] * 4,
        out_shape=[jax.ShapeDtypeStruct((128, SLAB), bf16)] * 4,
        compiler_params=PARAMS,
        cost_estimate=cost(0, 4_700_000),
        name="slab_in",
    )(scalars, q, k, v)


def slab_out_kernel(scalars, o_ref, *outs):
    for k, out in enumerate(outs):
        at = lax.rem(scalars[1] + k, 4) * COLS
        for s in range(16):
            out[:, COLS * s : COLS * s + COLS] = o_ref[
                0, :, pl.ds(pl.multiple_of(at + 1024 * s, COLS), COLS)
            ]


def slab_out(layer, scalars, o):
    return pl.pallas_call(
        slab_out_kernel,
        grid=(4,),
        in_specs=[SMEM, pl.BlockSpec((1, 16, WIDTH), lambda s: (layer, s, 0))],
        out_specs=[pl.BlockSpec((16, OCOLS), lambda s: (s, 0))] * 4,
        out_shape=[jax.ShapeDtypeStruct((64, OCOLS), bf16)] * 4,
        compiler_params=PARAMS,
        cost_estimate=cost(0, 4_200_000),
        name="slab_out",
    )(scalars, o)


def project_kernel(layer, scalars, *refs):
    xs, gain_ref, ws, kvs, refs = refs[:4], refs[4], refs[5:13], refs[13:21], refs[21:]
    out_ref, xg_ref, ss_ref, kv_ref = refs
    z, core = scalars[0], scalars[2]

    @pl.when(pl.program_id(0) == 0)
    def _():
        gains = gain_ref[lax.rem(z - layer + 4, 4)]
        at = lax.broadcasted_iota(jnp.int32, (4, COLS), 0)
        total = jnp.zeros((SEQ, 1), f32)
        parts = []
        for k in range(4):
            wide = xs[k][...].astype(f32)
            total += jnp.sum(wide * wide, axis=1, keepdims=True)
            gain = jnp.sum(jnp.where(at == lax.rem(z - k + 4, 4), gains, 0.0), axis=0, keepdims=True)
            scaled = wide * gain
            turned = jnp.concatenate([scaled[:, 128:], scaled[:, :128]], axis=1)
            parts.append(jnp.where(core == 1, turned, scaled))
        scaled = jnp.concatenate(parts, axis=1)
        xg_ref[...] = scaled.astype(bf16)
        padded = jnp.concatenate([scaled, jnp.zeros((128 - SEQ, 1024), f32)], axis=0).astype(bf16)
        eye, _ = masks()
        row = jnp.sum(jnp.where(eye, total, 0.0), axis=0, keepdims=True)
        high = row.astype(bf16).astype(f32)
        which = lax.broadcasted_iota(jnp.int32, (8, 128), 0)
        ss_ref[...] = jnp.where(which == 0, high, jnp.where(which == 1, row - high, 0.0))
        kv = dot(padded, jnp.concatenate([w[...] for w in kvs], axis=0))
        kv_ref[:128] = kv[:, :128].T
        kv_ref[128:] = kv[:, 128:].T

    q = dot(xg_ref[...], jnp.concatenate([w[...] for w in ws], axis=0))
    for h in range(4):
        out_ref[h] = jnp.concatenate(
            [kv_ref[...], ss_ref[...], q[:, HEAD * h : HEAD * h + HEAD]], axis=0
        ).astype(bf16)


def project(layer, scalars, xs, gains, weights):
    return pl.pallas_call(
        functools.partial(project_kernel, layer),
        grid=(4,),
        in_specs=[SMEM]
        + [whole(SEQ, COLS)] * 4
        + [whole(4, 4, COLS)]
        + [pl.BlockSpec((128, 512), lambda s: (0, s))] * 8
        + [pl.BlockSpec((128, 256), lambda s: (0, 8))] * 8,
        out_specs=pl.BlockSpec((4, ROWS, 128), lambda s: (s, 0, 0)),
        out_shape=jax.ShapeDtypeStruct((16, ROWS, 128), bf16),
        scratch_shapes=[
            pltpu.VMEM((SEQ, 1024), bf16),
            pltpu.VMEM((8, 128), f32),
            pltpu.VMEM((256, 128), f32),
        ],
        compiler_params=PARAMS,
        cost_estimate=cost(2 * SEQ * 1024 * SLAB, 6_500_000),
        name="project",
    )(scalars, *xs, gains, *weights, *weights)


def attend_kernel(recv_ref, out_ref, acc):
    step = pl.program_id(0)

    @pl.when(step == 0)
    def _():
        acc[...] = jnp.sum(recv_ref[...].astype(f32), axis=0)

    @pl.when(step > 0)
    def _():
        acc[...] += jnp.sum(recv_ref[...].astype(f32), axis=0)

    @pl.when(step == 3)
    def _():
        total = acc[256:257] + acc[257:258]
        row = lax.rsqrt(total * (1.0 / WIDTH) + 1e-05)
        eye, causal = masks()
        column = jnp.sum(jnp.where(eye, row, 0.0), axis=1, keepdims=True)
        q = (acc[264:] * column).astype(bf16)
        keys = (acc[:128] * row).astype(bf16)
        values = (acc[128:256] * row).astype(bf16)
        scores = dot(q, keys) * (1.0 / math.sqrt(HEAD))
        weights = jnp.where(causal, jnp.exp(scores), 0.0)
        shares = (weights / jnp.sum(weights, axis=1, keepdims=True)).astype(bf16)
        out_ref[...] = dot(shares, values, ((1,), (1,))).astype(bf16)


def attend(received):
    return pl.pallas_call(
        attend_kernel,
        grid=(4,),
        in_specs=[pl.BlockSpec((4, ROWS, 128), lambda s: (s, 0, 0))],
        out_specs=whole(SEQ, HEAD),
        out_shape=jax.ShapeDtypeStruct((SEQ, HEAD), bf16),
        scratch_shapes=[pltpu.VMEM((ROWS, 128), f32)],
        compiler_params=PARAMS,
        cost_estimate=cost(6_000_000, 1_500_000),
        name="attend",
    )(received)


def output_kernel(scalars, *refs):
    mixed, ws, out_ref, mixed_ref = refs[:4], refs[4:12], refs[12], refs[13]

    @pl.when(pl.program_id(0) == 0)
    def _():
        parts = []
        for part in mixed:
            part = part[...].astype(f32)
            turned = jnp.concatenate([part[:, 64:], part[:, :64]], axis=1)
            parts.append(jnp.where(scalars[2] == 1, turned, part))
        mixed_ref[...] = jnp.concatenate(parts, axis=1).astype(bf16)

    o = dot(mixed_ref[...], jnp.concatenate([w[...] for w in ws], axis=0))
    for i in range(4):
        out_ref[i] = o[:, COLS * i : COLS * i + COLS].astype(bf16)


def output(scalars, mixed, weights):
    return pl.pallas_call(
        output_kernel,
        grid=(4,),
        in_specs=[SMEM]
        + [whole(SEQ, HEAD)] * 4
        + [pl.BlockSpec((64, 1024), lambda s: (0, s))] * 8,
        out_specs=pl.BlockSpec((4, SEQ, COLS), lambda s: (s, 0, 0)),
        out_shape=jax.ShapeDtypeStruct((16, SEQ, COLS), bf16),
        scratch_shapes=[pltpu.VMEM((SEQ, 512), bf16)],
        compiler_params=PARAMS,
        cost_estimate=cost(2 * SEQ * 512 * OCOLS, 5_000_000),
        name="output",
    )(scalars, *mixed, *weights)


def close_kernel(recv_ref, x_ref, out_ref):
    out_ref[...] = (x_ref[...].astype(f32) + jnp.sum(recv_ref[...].astype(f32), axis=0)).astype(bf16)


def close(received, x):
    return pl.pallas_call(
        close_kernel,
        grid=(1,),
        in_specs=[whole(16, SEQ, COLS), whole(SEQ, COLS)],
        out_specs=whole(SEQ, COLS),
        out_shape=jax.ShapeDtypeStruct((SEQ, COLS), bf16),
        compiler_params=PARAMS,
        cost_estimate=cost(400_000, 800_000),
        name="close",
    )(received, x)


def exchange(value, axes):
    return lax.all_to_all(value, axes, 0, 0, tiled=True)


def shift(value, axis, by):
    return lax.ppermute(value, axis, [(i, (i + by) % 4) for i in range(4)])


def line(value, axis):
    return [value] + [shift(value, axis, k) for k in range(1, 4)]


def after(gate, values):
    return lax.optimization_barrier((gate, values))


def relay(slabs, axis):
    return [slabs[0]] + [shift(slabs[k], axis, k) for k in range(1, 4)]


def swapped(pieces):
    others = [lax.ppermute(piece, "c", [(0, 1), (1, 0)]) for piece in pieces]
    return [side for pair in zip(pieces, others) for side in pair]


def body(entering, norm_gain, query_weight, key_matrix, value_matrix, output_weight):
    plane, across, along, core = (lax.axis_index(name) for name in ALL)
    slot = 2 * core + lax.rem(along, 2)
    scalars = jnp.stack([plane, along, core]).astype(jnp.int32)

    rounds = []
    for r in range(4):
        pairs = []
        for p in range(4):
            for t in range(32):
                s = (t // 8 - r) % 4
                pairs.append((32 * p + t, 32 * p + 2 * ((2 * t) % 16 + s % 2) + s // 2))
        s = lax.rem(across - r + 4, 4)
        piece = lax.dynamic_slice(entering, (s // 2, 0, lax.rem(s, 2) * COLS), (1, SEQ, COLS))[0]
        gain = lax.dynamic_slice(norm_gain, (0, lax.rem(s, 2) * COLS), (1, COLS))
        piece = jnp.concatenate([piece, jnp.broadcast_to(gain, (8, COLS))], axis=0)
        rounds.append(lax.ppermute(piece, ALL, pairs))
    rounds = jnp.stack(rounds)
    xs = [
        lax.dynamic_index_in_dim(rounds, lax.rem(plane - k - slot + 8, 4), 0, keepdims=False)[:SEQ]
        for k in range(4)
    ]
    gains = jnp.stack([rounds[:, SEQ][lax.rem(p - slot + 4, 4)] for p in range(4)])
    gains = jnp.stack(line(gains, "z")).astype(f32)

    slabs = [slab_in(layer, scalars, query_weight, key_matrix, value_matrix) for layer in range(4)]
    cuts = [slab_out(layer, scalars, output_weight) for layer in range(4)]
    ins = swapped(relay(slabs[0], "z"))
    outs = relay(cuts[0], "y")
    xs, (slabs, cuts) = after(xs, (slabs[1:], cuts[1:]))
    states = []
    for layer in range(4):
        xs, outs = after(xs, outs)
        partial = project(layer, scalars, xs, gains, ins)
        partial, outs = after(partial, outs)
        if layer < 3:
            partial, slab = after(partial, slabs[layer])
            ins = relay(slab, "z")
        outs = swapped(outs)
        mixed = line(attend(exchange(partial, ("x", "y"))), "y")
        if layer < 3:
            mixed, ins = after(mixed, ins)
        partial = output(scalars, mixed, outs)
        if layer < 3:
            partial, (ins, cut) = after(partial, (ins, cuts[layer]))
            ins = swapped(ins)
            outs = relay(cut, "y")
        x = close(exchange(partial, ("z", "x")), xs[0])
        states.append(x)
        if layer < 3:
            xs = line(x, "z")

    states = jnp.stack(states)
    rounds = []
    for k in range(4):
        pairs = [
            (2 * i + c, 32 * ((2 * c + i % 2 + k) % 4) + i // 2) for i in range(64) for c in range(2)
        ]
        piece = lax.dynamic_index_in_dim(states, lax.rem(slot + k, 4), 0, keepdims=False)
        rounds.append(lax.ppermute(piece, ALL, pairs))
    rounds = jnp.stack(rounds)
    pieces = [
        lax.dynamic_index_in_dim(rounds, lax.rem(plane - s + 4, 4), 0, keepdims=False) for s in range(4)
    ]
    return jnp.stack(
        [jnp.concatenate(pieces[:2], axis=1), jnp.concatenate(pieces[2:], axis=1)]
    )[None]


def solution(mesh):
    fine = Mesh(mesh.devices.reshape(4, 4, 4, 2), ALL)
    tp = ("x", "y", "c")
    rows = P(None, ALL, None)
    return jax.shard_map(
        body,
        mesh=fine,
        in_specs=(P(None, None, tp), P("z", tp), rows, rows, rows, rows),
        out_specs=P("z", None, None, tp),
        check_vma=False,
    )
```

```python
import functools
import math

import jax
import jax.numpy as jnp
from jax import lax
from jax.experimental import pallas as pl
from jax.experimental.pallas import tpu as pltpu
from jax.sharding import Mesh, PartitionSpec as P


ALL = ("z", "x", "y", "c")
HEAD = 128
SEQ = 88
COLS = 256
WIDTH = 16384
SLAB = 2304
OCOLS = 4096
ROWS = 352
VMEM_LIMIT = 48 * 1024 * 1024
f32 = jnp.float32
bf16 = jnp.bfloat16
SMEM = pl.BlockSpec(memory_space=pltpu.SMEM)
PARAMS = pltpu.CompilerParams(vmem_limit_bytes=VMEM_LIMIT)


def dot(a, b, contract=((1,), (0,))):
    return lax.dot_general(a, b, (contract, ((), ())), preferred_element_type=f32)


def whole(*shape):
    return pl.BlockSpec(shape, lambda s: (0,) * len(shape))


def cost(flops, size):
    return pl.CostEstimate(flops=flops, bytes_accessed=size, transcendentals=0)


def masks():
    rows = lax.broadcasted_iota(jnp.int32, (SEQ, 128), 0)
    lanes = lax.broadcasted_iota(jnp.int32, (SEQ, 128), 1)
    return rows == lanes, lanes <= rows


def slab_in_kernel(scalars, q_ref, k_ref, v_ref, *outs):
    for k, out in enumerate(outs):
        at = lax.bitwise_xor(scalars[0], k)
        out[:, :2048] = q_ref[0, :, pl.ds(pl.multiple_of(at * 2048, 2048), 2048)]
        out[:, 2048:2176] = k_ref[0, :, pl.ds(pl.multiple_of(at * 128, 128), 128)]
        out[:, 2176:] = v_ref[0, :, pl.ds(pl.multiple_of(at * 128, 128), 128)]


def slab_in(layer, scalars, q, k, v):
    return pl.pallas_call(
        slab_in_kernel,
        grid=(2,),
        in_specs=[
            SMEM,
            pl.BlockSpec((1, 64, 8192), lambda s: (layer, s, 0)),
            pl.BlockSpec((1, 64, 512), lambda s: (layer, s, 0)),
            pl.BlockSpec((1, 64, 512), lambda s: (layer, s, 0)),
        ],
        out_specs=[pl.BlockSpec((64, SLAB), lambda s: (s, 0))] * 4,
        out_shape=[pltpu.HBM((128, SLAB), bf16)] * 4,
        compiler_params=PARAMS,
        cost_estimate=cost(0, 4_700_000),
        name="slab_in",
    )(scalars, q, k, v)


def slab_out_kernel(scalars, o_ref, *outs):
    for k, out in enumerate(outs):
        at = lax.bitwise_xor(scalars[1], k) * COLS
        for s in range(16):
            out[:, COLS * s : COLS * s + COLS] = o_ref[
                0, :, pl.ds(pl.multiple_of(at + 1024 * s, COLS), COLS)
            ]


def slab_out(layer, scalars, o):
    return pl.pallas_call(
        slab_out_kernel,
        grid=(2,),
        in_specs=[SMEM, pl.BlockSpec((1, 32, WIDTH), lambda s: (layer, s, 0))],
        out_specs=[pl.BlockSpec((32, OCOLS), lambda s: (s, 0))] * 4,
        out_shape=[pltpu.HBM((64, OCOLS), bf16)] * 4,
        compiler_params=PARAMS,
        cost_estimate=cost(0, 4_200_000),
        name="slab_out",
    )(scalars, o)


def join_kernel(*refs):
    for k, ref in enumerate(refs[:4]):
        refs[4][k] = ref[...]


def join(pieces):
    rows, columns = pieces[0].shape
    half = rows // 2
    return pl.pallas_call(
        join_kernel,
        grid=(2,),
        in_specs=[pl.BlockSpec((half, columns), lambda s: (s, 0))] * 4,
        out_specs=pl.BlockSpec((4, half, columns), lambda s: (0, s, 0)),
        out_shape=pltpu.HBM((4, rows, columns), bf16),
        compiler_params=PARAMS,
        cost_estimate=cost(0, 4_500_000),
        name="join",
    )(*pieces)


def project_kernel(layer, scalars, *refs):
    xs, pieces, refs = refs[:4], refs[4:8], refs[8:]
    gain_ref, own, other, kv_own, kv_other, out_ref, joined_ref, xg_ref, ss_ref, kv_ref = refs
    z, core = scalars[0], scalars[2]
    for k in range(4):
        joined_ref[k] = pieces[k][...]

    @pl.when(pl.program_id(0) == 0)
    def _():
        at = lax.broadcasted_iota(jnp.int32, (4, COLS), 0) == lax.bitwise_xor(z, layer)
        total = jnp.zeros((SEQ, 1), f32)
        low, high = [], []
        for k in range(4):
            wide = xs[k][...].astype(f32)
            total += jnp.sum(wide * wide, axis=1, keepdims=True)
            scaled = wide * jnp.sum(jnp.where(at, gain_ref[k], 0.0), axis=0, keepdims=True)
            low.append(scaled[:, :128])
            high.append(scaled[:, 128:])
        scaled = jnp.where(
            core == 1, jnp.concatenate(high + low, axis=1), jnp.concatenate(low + high, axis=1)
        )
        xg_ref[...] = scaled.astype(bf16)
        padded = jnp.concatenate([scaled, jnp.zeros((128 - SEQ, 1024), f32)], axis=0).astype(bf16)
        eye, _ = masks()
        row = jnp.sum(jnp.where(eye, total, 0.0), axis=0, keepdims=True)
        coarse = row.astype(bf16).astype(f32)
        which = lax.broadcasted_iota(jnp.int32, (8, 128), 0)
        ss_ref[...] = jnp.where(which == 0, coarse, jnp.where(which == 1, row - coarse, 0.0))
        kv = dot(padded[:, :512], kv_own[...].reshape(512, 256))
        kv += dot(padded[:, 512:], kv_other[...].reshape(512, 256))
        kv_ref[:128] = kv[:, :128].T
        kv_ref[128:] = kv[:, 128:].T

    q = dot(xg_ref[:, :512], own[...].reshape(512, 512))
    q += dot(xg_ref[:, 512:], other[...].reshape(512, 512))
    for h in range(4):
        out_ref[h] = jnp.concatenate(
            [kv_ref[...], ss_ref[...], q[:, HEAD * h : HEAD * h + HEAD]], axis=0
        ).astype(bf16)


def project(layer, scalars, xs, gains, weights, pieces):
    return pl.pallas_call(
        functools.partial(project_kernel, layer),
        grid=(4,),
        in_specs=[SMEM]
        + [whole(SEQ, COLS)] * 4
        + [pl.BlockSpec((64, 1024), lambda s: (0, s))] * 4
        + [whole(4, 4, COLS)]
        + [pl.BlockSpec((4, 128, 512), lambda s: (0, 0, s))] * 2
        + [pl.BlockSpec((4, 128, 256), lambda s: (0, 0, 8))] * 2,
        out_specs=[
            pl.BlockSpec((4, ROWS, 128), lambda s: (s, 0, 0)),
            pl.BlockSpec((4, 64, 1024), lambda s: (0, 0, s)),
        ],
        out_shape=[pltpu.HBM((16, ROWS, 128), bf16), pltpu.HBM((4, 64, OCOLS), bf16)],
        scratch_shapes=[
            pltpu.VMEM((SEQ, 1024), bf16),
            pltpu.VMEM((8, 128), f32),
            pltpu.VMEM((256, 128), f32),
        ],
        compiler_params=PARAMS,
        cost_estimate=cost(2 * SEQ * 1024 * SLAB, 10_000_000),
        name="project",
    )(scalars, *xs, *pieces, gains, *weights, *weights)


def attend_kernel(recv_ref, out_ref, acc):
    step = pl.program_id(0)

    @pl.when(step == 0)
    def _():
        acc[...] = jnp.sum(recv_ref[...].astype(f32), axis=0)

    @pl.when(step > 0)
    def _():
        acc[...] += jnp.sum(recv_ref[...].astype(f32), axis=0)

    @pl.when(step == 3)
    def _():
        total = acc[256:257] + acc[257:258]
        row = lax.rsqrt(total * (1.0 / WIDTH) + 1e-05)
        eye, causal = masks()
        column = jnp.sum(jnp.where(eye, row, 0.0), axis=1, keepdims=True)
        q = (acc[264:] * column).astype(bf16)
        keys = (acc[:128] * row).astype(bf16)
        values = (acc[128:256] * row).astype(bf16)
        scores = dot(q, keys) * (1.0 / math.sqrt(HEAD))
        weights = jnp.where(causal, jnp.exp(scores), 0.0)
        shares = (weights / jnp.sum(weights, axis=1, keepdims=True)).astype(bf16)
        out_ref[...] = dot(shares, values, ((1,), (1,))).astype(bf16)


def attend(received):
    return pl.pallas_call(
        attend_kernel,
        grid=(4,),
        in_specs=[pl.BlockSpec((4, ROWS, 128), lambda s: (s, 0, 0))],
        out_specs=whole(SEQ, HEAD),
        out_shape=jax.ShapeDtypeStruct((SEQ, HEAD), bf16),
        scratch_shapes=[pltpu.VMEM((ROWS, 128), f32)],
        compiler_params=PARAMS,
        cost_estimate=cost(6_000_000, 1_500_000),
        name="attend",
    )(received)


def output_kernel(scalars, *refs):
    mixed, own, other, mixed_ref = refs[:4], refs[4], refs[5], refs[-1]
    if len(refs) == 8:
        out_ref = refs[6]
    else:
        pieces, out_ref, joined_ref = refs[6:10], refs[10], refs[11]
        for k in range(4):
            joined_ref[k] = pieces[k][...]

    @pl.when(pl.program_id(0) == 0)
    def _():
        parts = [part[...].astype(f32) for part in mixed]
        low, high = [part[:, :64] for part in parts], [part[:, 64:] for part in parts]
        mixed_ref[...] = jnp.where(
            scalars[2] == 1, jnp.concatenate(high + low, axis=1), jnp.concatenate(low + high, axis=1)
        ).astype(bf16)

    o = dot(mixed_ref[:, :256], own[...].reshape(256, 1024))
    o += dot(mixed_ref[:, 256:], other[...].reshape(256, 1024))
    for i in range(4):
        out_ref[i] = o[:, COLS * i : COLS * i + COLS].astype(bf16)


def output(scalars, mixed, weights, pieces):
    specs = [SMEM] + [whole(SEQ, HEAD)] * 4 + [pl.BlockSpec((4, 64, 1024), lambda s: (0, 0, s))] * 2
    outs = [pltpu.HBM((16, SEQ, COLS), bf16)]
    out_specs = [pl.BlockSpec((4, SEQ, COLS), lambda s: (s, 0, 0))]
    if pieces:
        specs += [pl.BlockSpec((32, SLAB), lambda s: (s, 0))] * 4
        outs.append(pltpu.HBM((4, 128, SLAB), bf16))
        out_specs.append(pl.BlockSpec((4, 32, SLAB), lambda s: (0, s, 0)))
    return pl.pallas_call(
        output_kernel,
        grid=(4,),
        in_specs=specs,
        out_specs=out_specs,
        out_shape=outs,
        scratch_shapes=[pltpu.VMEM((SEQ, 512), bf16)],
        compiler_params=PARAMS,
        cost_estimate=cost(2 * SEQ * 512 * OCOLS, 10_000_000),
        name="output",
    )(scalars, *mixed, *weights, *pieces)


def close_kernel(recv_ref, x_ref, out_ref):
    out_ref[...] = (x_ref[...].astype(f32) + jnp.sum(recv_ref[...].astype(f32), axis=0)).astype(bf16)


def close(received, x):
    return pl.pallas_call(
        close_kernel,
        grid=(1,),
        in_specs=[whole(16, SEQ, COLS), whole(SEQ, COLS)],
        out_specs=whole(SEQ, COLS),
        out_shape=jax.ShapeDtypeStruct((SEQ, COLS), bf16),
        compiler_params=PARAMS,
        cost_estimate=cost(400_000, 800_000),
        name="close",
    )(received, x)


def exchange(value, axes):
    return lax.all_to_all(value, axes, 0, 0, tiled=True)


def across_line(value, axis, by):
    return lax.ppermute(value, axis, [(i, i ^ by) for i in range(4)])


def line(value, axis):
    near, far = (across_line(value, axis, by) for by in (1, 2))
    return [value, near, far, across_line(near, axis, 2)]


def after(gate, values):
    return lax.optimization_barrier((gate, values))


def relay(slabs, axis):
    return [slabs[0]] + [across_line(slabs[k], axis, k) for k in range(1, 4)]


def swapped(joined):
    return joined, lax.ppermute(joined, "c", [(0, 1), (1, 0)])


def body(entering, norm_gain, query_weight, key_matrix, value_matrix, output_weight):
    plane, across, along, core = (lax.axis_index(name) for name in ALL)
    slot = 2 * core + lax.rem(along, 2)
    scalars = jnp.stack([plane, along, core]).astype(jnp.int32)

    gains = jnp.concatenate(line(norm_gain, "z"), axis=0)
    slab = slab_in(0, scalars, query_weight, key_matrix, value_matrix)
    gains, slab = after(gains, slab)
    ins = relay(slab, "z")

    rounds = []
    for r in range(4):
        pairs = []
        for p in range(4):
            for t in range(32):
                s = (t // 8 - r) % 4
                pairs.append((32 * p + t, 32 * p + 2 * ((2 * t) % 16 + s % 2) + s // 2))
        s = lax.rem(across - r + 4, 4)
        piece = lax.dynamic_slice(entering, (s // 2, 0, lax.rem(s, 2) * COLS), (1, SEQ, COLS))[0]
        gain = lax.dynamic_slice(gains, (0, lax.rem(s, 2) * COLS), (4, COLS))
        piece = jnp.concatenate([piece, gain, gain], axis=0)
        rounds.append(lax.ppermute(piece, ALL, pairs))
    rounds = jnp.stack(rounds)
    rounds, scalars = after(rounds, scalars)
    cut = slab_out(0, scalars, output_weight)
    outs = relay(cut, "y")
    lines = [
        lax.dynamic_index_in_dim(rounds, lax.rem(lax.bitwise_xor(plane, k) - slot + 4, 4), 0, keepdims=False)
        for k in range(4)
    ]
    xs = [part[:SEQ] for part in lines]
    gains = jnp.stack([part[SEQ : SEQ + 4] for part in lines]).astype(f32)

    slabs = [slab_in(layer, scalars, query_weight, key_matrix, value_matrix) for layer in range(1, 4)]
    cuts = [slab_out(layer, scalars, output_weight) for layer in range(1, 4)]
    ins, (outs, slabs, cuts) = after(ins, (outs, slabs, cuts))
    ins = swapped(join(ins))
    states = []
    for layer in range(4):
        xs, outs = after(xs, outs)
        partial, outs = project(layer, scalars, xs, gains, ins, outs)
        if layer < 3:
            partial, slab = after(partial, slabs[layer])
            ins = relay(slab, "z")
        received, outs = after(exchange(partial, ("x", "y")), swapped(outs))
        mixed = line(attend(received), "y")
        if layer < 3:
            mixed, ins = after(mixed, ins)
            partial, ins = output(scalars, mixed, outs, ins)
            partial, cut = after(partial, cuts[layer])
            outs = relay(cut, "y")
            ins = swapped(ins)
        else:
            partial = output(scalars, mixed, outs, [])[0]
        x = close(exchange(partial, ("z", "x")), xs[0])
        states.append(x)
        if layer < 3:
            xs = line(x, "z")

    states = jnp.stack(states)
    rounds = []
    for k in range(4):
        pairs = [
            (2 * i + c, 32 * ((2 * c + i % 2 + k) % 4) + i // 2) for i in range(64) for c in range(2)
        ]
        piece = lax.dynamic_index_in_dim(states, lax.rem(slot + k, 4), 0, keepdims=False)
        rounds.append(lax.ppermute(piece, ALL, pairs))
    rounds = jnp.stack(rounds)
    pieces = [
        lax.dynamic_index_in_dim(rounds, lax.rem(plane - s + 4, 4), 0, keepdims=False) for s in range(4)
    ]
    return jnp.stack(
        [jnp.concatenate(pieces[:2], axis=1), jnp.concatenate(pieces[2:], axis=1)]
    )[None]


def solution(mesh):
    fine = Mesh(mesh.devices.reshape(4, 4, 4, 2), ALL)
    tp = ("x", "y", "c")
    rows = P(None, ALL, None)
    return jax.shard_map(
        body,
        mesh=fine,
        in_specs=(P(None, None, tp), P("z", tp), rows, rows, rows, rows),
        out_specs=P("z", None, None, tp),
        check_vma=False,
    )
```

```python
import functools
import math

import jax
import jax.numpy as jnp
from jax import lax
from jax.experimental import pallas as pl
from jax.experimental.pallas import tpu as pltpu
from jax.sharding import Mesh, PartitionSpec as P


ALL = ("z", "x", "y", "c")
HEAD = 128
SEQ = 88
COLS = 256
WIDTH = 16384
SLAB = 2304
OCOLS = 4096
ROWS = 272
VMEM_LIMIT = 52 * 1024 * 1024
f32 = jnp.float32
bf16 = jnp.bfloat16
SMEM = pl.BlockSpec(memory_space=pltpu.SMEM)
PARAMS = pltpu.CompilerParams(vmem_limit_bytes=VMEM_LIMIT)


def dot(a, b, contract=((1,), (0,))):
    return lax.dot_general(a, b, (contract, ((), ())), preferred_element_type=f32)


def whole(*shape):
    return pl.BlockSpec(shape, lambda s: (0,) * len(shape))


def cost(flops, size):
    return pl.CostEstimate(flops=flops, bytes_accessed=size, transcendentals=0)


def masks():
    rows = lax.broadcasted_iota(jnp.int32, (SEQ, 128), 0)
    lanes = lax.broadcasted_iota(jnp.int32, (SEQ, 128), 1)
    return rows == lanes, lanes <= rows


def slab_in_kernel(scalars, q_ref, k_ref, v_ref, *outs):
    for k, out in enumerate(outs):
        at = lax.bitwise_xor(scalars[0], k)
        out[:, :2048] = q_ref[0, :, pl.ds(pl.multiple_of(at * 2048, 2048), 2048)]
        out[:, 2048:2176] = k_ref[0, :, pl.ds(pl.multiple_of(at * 128, 128), 128)]
        out[:, 2176:] = v_ref[0, :, pl.ds(pl.multiple_of(at * 128, 128), 128)]


def slab_in(layer, scalars, q, k, v):
    return pl.pallas_call(
        slab_in_kernel,
        grid=(2,),
        in_specs=[
            SMEM,
            pl.BlockSpec((1, 64, 8192), lambda s: (layer, s, 0)),
            pl.BlockSpec((1, 64, 512), lambda s: (layer, s, 0)),
            pl.BlockSpec((1, 64, 512), lambda s: (layer, s, 0)),
        ],
        out_specs=[pl.BlockSpec((64, SLAB), lambda s: (s, 0))] * 4,
        out_shape=[pltpu.HBM((128, SLAB), bf16)] * 4,
        compiler_params=PARAMS,
        cost_estimate=cost(0, 4_700_000),
        name="slab_in",
    )(scalars, q, k, v)


def slab_out_kernel(scalars, o_ref, *outs):
    for k, out in enumerate(outs):
        at = lax.bitwise_xor(scalars[1], k) * COLS
        for s in range(16):
            out[:, COLS * s : COLS * s + COLS] = o_ref[
                0, :, pl.ds(pl.multiple_of(at + 1024 * s, COLS), COLS)
            ]


def slab_out(layer, scalars, o):
    return pl.pallas_call(
        slab_out_kernel,
        grid=(2,),
        in_specs=[SMEM, pl.BlockSpec((1, 32, WIDTH), lambda s: (layer, s, 0))],
        out_specs=[pl.BlockSpec((32, OCOLS), lambda s: (s, 0))] * 4,
        out_shape=[pltpu.HBM((64, OCOLS), bf16)] * 4,
        compiler_params=PARAMS,
        cost_estimate=cost(0, 4_200_000),
        name="slab_out",
    )(scalars, o)


def join_kernel(*refs):
    for k, ref in enumerate(refs[:4]):
        refs[4][k] = ref[...]


def join(pieces):
    rows, columns = pieces[0].shape
    half = rows // 2
    return pl.pallas_call(
        join_kernel,
        grid=(2,),
        in_specs=[pl.BlockSpec((half, columns), lambda s: (s, 0))] * 4,
        out_specs=pl.BlockSpec((4, half, columns), lambda s: (0, s, 0)),
        out_shape=pltpu.HBM((4, rows, columns), bf16),
        compiler_params=PARAMS,
        cost_estimate=cost(0, 4_500_000),
        name="join",
    )(*pieces)


def project_kernel(layer, scalars, *refs):
    xs, pieces, refs = refs[:4], refs[4:8], refs[8:]
    gain_ref, own, other, kv_own, kv_other, out_ref, joined_ref, xg_ref, lead_ref = refs
    z, core = scalars[0], scalars[2]
    for k in range(4):
        joined_ref[k] = pieces[k][...]

    @pl.when(pl.program_id(0) == 0)
    def _():
        rows = lax.broadcasted_iota(jnp.int32, (4, COLS), 0)
        gains = gain_ref[lax.bitwise_xor(z, layer)]
        total = jnp.zeros((SEQ, 1), f32)
        low, high = [], []
        for k in range(4):
            wide = xs[k][...].astype(f32)
            total += jnp.sum(wide * wide, axis=1, keepdims=True)
            at = rows == lax.bitwise_xor(z, k)
            scaled = wide * jnp.sum(jnp.where(at, gains, 0.0), axis=0, keepdims=True)
            low.append(scaled[:, :128])
            high.append(scaled[:, 128:])
        xg_ref[...] = jnp.where(
            core == 1, jnp.concatenate(high + low, axis=1), jnp.concatenate(low + high, axis=1)
        ).astype(bf16)
        eye, _ = masks()
        row = jnp.sum(jnp.where(eye, total, 0.0), axis=0, keepdims=True)
        coarse = row.astype(bf16).astype(f32)
        which = lax.broadcasted_iota(jnp.int32, (8, 128), 0)
        lead_ref[:8] = jnp.where(which == 0, coarse, jnp.where(which == 1, row - coarse, 0.0))
        kv = dot(xg_ref[:, :512], kv_own[...].reshape(512, 256))
        kv += dot(xg_ref[:, 512:], kv_other[...].reshape(512, 256))
        lead_ref[8 : 8 + SEQ] = kv[:, :128]
        lead_ref[8 + SEQ :] = kv[:, 128:]

    q = dot(xg_ref[:, :512], own[...].reshape(512, 512))
    q += dot(xg_ref[:, 512:], other[...].reshape(512, 512))
    for h in range(4):
        out_ref[h] = jnp.concatenate(
            [lead_ref[...], q[:, HEAD * h : HEAD * h + HEAD]], axis=0
        ).astype(bf16)


def project(layer, scalars, xs, gains, weights, pieces):
    return pl.pallas_call(
        functools.partial(project_kernel, layer),
        grid=(4,),
        in_specs=[SMEM]
        + [whole(SEQ, COLS)] * 4
        + [pl.BlockSpec((64, 1024), lambda s: (0, s))] * 4
        + [whole(4, 4, COLS)]
        + [pl.BlockSpec((4, 128, 512), lambda s: (0, 0, s))] * 2
        + [pl.BlockSpec((4, 128, 256), lambda s: (0, 0, 8))] * 2,
        out_specs=[
            pl.BlockSpec((4, ROWS, 128), lambda s: (s, 0, 0)),
            pl.BlockSpec((4, 64, 1024), lambda s: (0, 0, s)),
        ],
        out_shape=[
            jax.ShapeDtypeStruct((16, ROWS, 128), bf16),
            jax.ShapeDtypeStruct((4, 64, OCOLS), bf16),
        ],
        scratch_shapes=[pltpu.VMEM((SEQ, 1024), bf16), pltpu.VMEM((8 + 2 * SEQ, 128), f32)],
        compiler_params=PARAMS,
        cost_estimate=cost(2 * SEQ * 1024 * SLAB, 6_000_000),
        name="project",
    )(scalars, *xs, *pieces, gains, *weights, *weights)


def attend_kernel(recv_ref, out_ref, acc):
    step = pl.program_id(0)

    @pl.when(step == 0)
    def _():
        acc[...] = jnp.sum(recv_ref[...].astype(f32), axis=0)

    @pl.when(step > 0)
    def _():
        acc[...] += jnp.sum(recv_ref[...].astype(f32), axis=0)

    @pl.when(step == 3)
    def _():
        row = lax.rsqrt((acc[0:1] + acc[1:2]) * (1.0 / WIDTH) + 1e-05)
        eye, _ = masks()
        column = jnp.sum(jnp.where(eye, row, 0.0), axis=1, keepdims=True)
        keys, values, queries = (
            (acc[8 + SEQ * k : 8 + SEQ * k + SEQ] * column).astype(bf16) for k in range(3)
        )
        scores = dot(queries, keys, ((1,), (1,))) * (1.0 / math.sqrt(HEAD))
        causal = lax.broadcasted_iota(jnp.int32, (SEQ, SEQ), 0) >= lax.broadcasted_iota(
            jnp.int32, (SEQ, SEQ), 1
        )
        weights = jnp.where(causal, jnp.exp(scores), 0.0)
        shares = (weights / jnp.sum(weights, axis=1, keepdims=True)).astype(bf16)
        out_ref[...] = dot(shares, values).astype(bf16)


def attend(received):
    return pl.pallas_call(
        attend_kernel,
        grid=(4,),
        in_specs=[pl.BlockSpec((4, ROWS, 128), lambda s: (s, 0, 0))],
        out_specs=whole(SEQ, HEAD),
        out_shape=jax.ShapeDtypeStruct((SEQ, HEAD), bf16),
        scratch_shapes=[pltpu.VMEM((ROWS, 128), f32)],
        compiler_params=PARAMS,
        cost_estimate=cost(6_000_000, 1_200_000),
        name="attend",
    )(received)


def output_kernel(scalars, *refs):
    mixed, own, other, mixed_ref = refs[:4], refs[4], refs[5], refs[-1]
    if len(refs) == 8:
        out_ref = refs[6]
    else:
        pieces, out_ref, joined_ref = refs[6:10], refs[10], refs[11]
        for k in range(4):
            joined_ref[k] = pieces[k][...]

    @pl.when(pl.program_id(0) == 0)
    def _():
        parts = [part[...].astype(f32) for part in mixed]
        low, high = [part[:, :64] for part in parts], [part[:, 64:] for part in parts]
        mixed_ref[...] = jnp.where(
            scalars[2] == 1, jnp.concatenate(high + low, axis=1), jnp.concatenate(low + high, axis=1)
        ).astype(bf16)

    o = dot(mixed_ref[:, :256], own[...].reshape(256, 1024))
    o += dot(mixed_ref[:, 256:], other[...].reshape(256, 1024))
    for i in range(4):
        out_ref[i] = o[:, COLS * i : COLS * i + COLS].astype(bf16)


def output(scalars, mixed, weights, pieces):
    specs = [SMEM] + [whole(SEQ, HEAD)] * 4 + [pl.BlockSpec((4, 64, 1024), lambda s: (0, 0, s))] * 2
    outs = [pltpu.HBM((16, SEQ, COLS), bf16)]
    out_specs = [pl.BlockSpec((4, SEQ, COLS), lambda s: (s, 0, 0))]
    if pieces:
        specs += [pl.BlockSpec((32, SLAB), lambda s: (s, 0))] * 4
        outs.append(pltpu.HBM((4, 128, SLAB), bf16))
        out_specs.append(pl.BlockSpec((4, 32, SLAB), lambda s: (0, s, 0)))
    return pl.pallas_call(
        output_kernel,
        grid=(4,),
        in_specs=specs,
        out_specs=out_specs,
        out_shape=outs,
        scratch_shapes=[pltpu.VMEM((SEQ, 512), bf16)],
        compiler_params=PARAMS,
        cost_estimate=cost(2 * SEQ * 512 * OCOLS, 10_000_000),
        name="output",
    )(scalars, *mixed, *weights, *pieces)


def close_kernel(recv_ref, x_ref, out_ref):
    out_ref[...] = (x_ref[...].astype(f32) + jnp.sum(recv_ref[...].astype(f32), axis=0)).astype(bf16)


def close(received, x):
    return pl.pallas_call(
        close_kernel,
        grid=(1,),
        in_specs=[whole(16, SEQ, COLS), whole(SEQ, COLS)],
        out_specs=whole(SEQ, COLS),
        out_shape=jax.ShapeDtypeStruct((SEQ, COLS), bf16),
        compiler_params=PARAMS,
        cost_estimate=cost(400_000, 800_000),
        name="close",
    )(received, x)


def exchange(value, axes):
    return lax.all_to_all(value, axes, 0, 0, tiled=True)


def across_line(value, axis, by):
    return lax.ppermute(value, axis, [(i, i ^ by) for i in range(4)])


def line(value, axis):
    near, far = (across_line(value, axis, by) for by in (1, 2))
    return [value, near, far, across_line(near, axis, 2)]


def after(gate, values):
    return lax.optimization_barrier((gate, values))


def relay(slabs, axis):
    return [slabs[0]] + [across_line(slabs[k], axis, k) for k in range(1, 4)]


def swapped(joined):
    return joined, lax.ppermute(joined, "c", [(0, 1), (1, 0)])


def body(entering, norm_gain, query_weight, key_matrix, value_matrix, output_weight):
    plane, across, along, core = (lax.axis_index(name) for name in ALL)
    slot = 2 * core + lax.rem(along, 2)
    scalars = jnp.stack([plane, along, core]).astype(jnp.int32)

    inward = lambda layer: slab_in(layer, scalars, query_weight, key_matrix, value_matrix)

    rounds = []
    for r in range(4):
        pairs = []
        for p in range(4):
            for t in range(32):
                s = (t // 8 - r) % 4
                pairs.append((32 * p + t, 32 * p + 2 * ((2 * t) % 16 + s % 2) + s // 2))
        s = lax.rem(across - r + 4, 4)
        piece = lax.dynamic_slice(entering, (s // 2, 0, lax.rem(s, 2) * COLS), (1, SEQ, COLS))[0]
        gain = lax.dynamic_slice(norm_gain, (0, lax.rem(s, 2) * COLS), (1, COLS))
        piece = jnp.concatenate([piece, jnp.broadcast_to(gain, (8, COLS))], axis=0)
        rounds.append(lax.ppermute(piece, ALL, pairs))
    rounds, (slab, cut) = after(rounds, (inward(0), slab_out(0, scalars, output_weight)))
    ins = relay(slab, "z")
    outs = relay(cut, "y")
    rounds = jnp.stack(rounds)
    xs = [
        lax.dynamic_index_in_dim(
            rounds, lax.rem(lax.bitwise_xor(plane, k) - slot + 4, 4), 0, keepdims=False
        )[:SEQ]
        for k in range(4)
    ]
    gains = jnp.stack(
        [
            lax.dynamic_index_in_dim(rounds[:, SEQ], lax.rem(p - slot + 4, 4), 0, keepdims=False)
            for p in range(4)
        ]
    )
    ahead = inward(1)
    ins, (outs, ahead, xs, gains) = after(ins, (outs, ahead, xs, gains))
    ins = swapped(join(ins))
    gains = jnp.stack(line(gains, "z")).astype(f32)
    states = []
    for layer in range(4):
        xs, outs = after(xs, outs)
        partial, outs = project(layer, scalars, xs, gains, ins, outs)
        if layer < 3:
            partial, (slab, scalars) = after(partial, (ahead, scalars))
            ins = relay(slab, "z")
            cut = slab_out(layer + 1, scalars, output_weight)
            if layer < 2:
                ahead = inward(layer + 2)
        received, outs = after(exchange(partial, ("x", "y")), swapped(outs))
        if layer < 3:
            received, (cut, ahead) = after(received, (cut, ahead))
        mixed = line(attend(received), "y")
        if layer < 3:
            mixed, (ins, cut) = after(mixed, (ins, cut))
            outs_next = relay(cut, "y")
            partial, ins = output(scalars, mixed, outs, ins)
            ins = swapped(ins)
            outs = outs_next
        else:
            partial = output(scalars, mixed, outs, [])[0]
        x = close(exchange(partial, ("z", "x")), xs[0])
        states.append(x)
        if layer < 3:
            xs = line(x, "z")

    states = jnp.stack(states)
    rounds = []
    for k in range(4):
        pairs = [
            (2 * i + c, 32 * ((2 * c + i % 2 + k) % 4) + i // 2) for i in range(64) for c in range(2)
        ]
        piece = lax.dynamic_index_in_dim(states, lax.rem(slot + k, 4), 0, keepdims=False)
        rounds.append(lax.ppermute(piece, ALL, pairs))
    rounds = jnp.stack(rounds)
    pieces = [
        lax.dynamic_index_in_dim(rounds, lax.rem(plane - s + 4, 4), 0, keepdims=False) for s in range(4)
    ]
    return jnp.stack(
        [jnp.concatenate(pieces[:2], axis=1), jnp.concatenate(pieces[2:], axis=1)]
    )[None]


def solution(mesh):
    fine = Mesh(mesh.devices.reshape(4, 4, 4, 2), ALL)
    tp = ("x", "y", "c")
    rows = P(None, ALL, None)
    return jax.shard_map(
        body,
        mesh=fine,
        in_specs=(P(None, None, tp), P("z", tp), rows, rows, rows, rows),
        out_specs=P("z", None, None, tp),
        check_vma=False,
    )
```

```python
import functools
import math

import jax
import jax.numpy as jnp
from jax import lax
from jax.experimental import pallas as pl
from jax.experimental.pallas import tpu as pltpu
from jax.sharding import Mesh, PartitionSpec as P


ALL = ("z", "x", "y", "c")
HEAD = 128
SEQ = 88
COLS = 256
WIDTH = 16384
SLAB = 2304
OCOLS = 4096
ROWS = 272
VMEM_LIMIT = 52 * 1024 * 1024
f32 = jnp.float32
bf16 = jnp.bfloat16
SMEM = pl.BlockSpec(memory_space=pltpu.SMEM)
PARAMS = pltpu.CompilerParams(vmem_limit_bytes=VMEM_LIMIT)


def dot(a, b, contract=((1,), (0,))):
    return lax.dot_general(a, b, (contract, ((), ())), preferred_element_type=f32)


def whole(*shape):
    return pl.BlockSpec(shape, lambda s: (0,) * len(shape))


def cost(flops, size):
    return pl.CostEstimate(flops=flops, bytes_accessed=size, transcendentals=0)


def masks():
    rows = lax.broadcasted_iota(jnp.int32, (SEQ, 128), 0)
    lanes = lax.broadcasted_iota(jnp.int32, (SEQ, 128), 1)
    return rows == lanes, lanes <= rows


def slab_in_kernel(scalars, q_ref, k_ref, v_ref, *outs):
    for k, out in enumerate(outs):
        at = lax.bitwise_xor(scalars[0], k)
        out[:, :2048] = q_ref[0, :, pl.ds(pl.multiple_of(at * 2048, 2048), 2048)]
        out[:, 2048:2176] = k_ref[0, :, pl.ds(pl.multiple_of(at * 128, 128), 128)]
        out[:, 2176:] = v_ref[0, :, pl.ds(pl.multiple_of(at * 128, 128), 128)]


def slab_in(layer, scalars, q, k, v):
    return pl.pallas_call(
        slab_in_kernel,
        grid=(2,),
        in_specs=[
            SMEM,
            pl.BlockSpec((1, 64, 8192), lambda s: (layer, s, 0)),
            pl.BlockSpec((1, 64, 512), lambda s: (layer, s, 0)),
            pl.BlockSpec((1, 64, 512), lambda s: (layer, s, 0)),
        ],
        out_specs=[pl.BlockSpec((64, SLAB), lambda s: (s, 0))] * 4,
        out_shape=[pltpu.HBM((128, SLAB), bf16)] * 4,
        compiler_params=PARAMS,
        cost_estimate=cost(0, 4_700_000),
        name="slab_in",
    )(scalars, q, k, v)


def slab_out_kernel(scalars, o_ref, *outs):
    for k, out in enumerate(outs):
        at = lax.bitwise_xor(scalars[1], k) * COLS
        for s in range(16):
            out[:, COLS * s : COLS * s + COLS] = o_ref[
                0, :, pl.ds(pl.multiple_of(at + 1024 * s, COLS), COLS)
            ]


def slab_out(layer, scalars, o):
    return pl.pallas_call(
        slab_out_kernel,
        grid=(2,),
        in_specs=[SMEM, pl.BlockSpec((1, 32, WIDTH), lambda s: (layer, s, 0))],
        out_specs=[pl.BlockSpec((32, OCOLS), lambda s: (s, 0))] * 4,
        out_shape=[pltpu.HBM((64, OCOLS), bf16)] * 4,
        compiler_params=PARAMS,
        cost_estimate=cost(0, 4_200_000),
        name="slab_out",
    )(scalars, o)


def join_kernel(*refs):
    for k, ref in enumerate(refs[:4]):
        refs[4][k] = ref[...]


def join(pieces):
    rows, columns = pieces[0].shape
    half = rows // 2
    return pl.pallas_call(
        join_kernel,
        grid=(2,),
        in_specs=[pl.BlockSpec((half, columns), lambda s: (s, 0))] * 4,
        out_specs=pl.BlockSpec((4, half, columns), lambda s: (0, s, 0)),
        out_shape=pltpu.HBM((4, rows, columns), bf16),
        compiler_params=PARAMS,
        cost_estimate=cost(0, 4_500_000),
        name="join",
    )(*pieces)


def project_kernel(layer, scalars, *refs):
    xs, pieces, refs = refs[:4], refs[4:8], refs[8:]
    gain_ref, own, other, kv_own, kv_other, out_ref, joined_ref, xg_ref, lead_ref = refs
    z, core = scalars[0], scalars[2]
    for k in range(4):
        joined_ref[k] = pieces[k][...]

    @pl.when(pl.program_id(0) == 0)
    def _():
        rows = lax.broadcasted_iota(jnp.int32, (4, COLS), 0)
        gains = gain_ref[lax.bitwise_xor(z, layer)]
        total = jnp.zeros((SEQ, 1), f32)
        low, high = [], []
        for k in range(4):
            wide = xs[k][...].astype(f32)
            total += jnp.sum(wide * wide, axis=1, keepdims=True)
            at = rows == lax.bitwise_xor(z, k)
            scaled = wide * jnp.sum(jnp.where(at, gains, 0.0), axis=0, keepdims=True)
            low.append(scaled[:, :128])
            high.append(scaled[:, 128:])
        xg_ref[...] = jnp.where(
            core == 1, jnp.concatenate(high + low, axis=1), jnp.concatenate(low + high, axis=1)
        ).astype(bf16)
        eye, _ = masks()
        row = jnp.sum(jnp.where(eye, total, 0.0), axis=0, keepdims=True)
        coarse = row.astype(bf16).astype(f32)
        which = lax.broadcasted_iota(jnp.int32, (8, 128), 0)
        lead_ref[:8] = jnp.where(which == 0, coarse, jnp.where(which == 1, row - coarse, 0.0))
        kv = dot(xg_ref[:, :512], kv_own[...].reshape(512, 256))
        kv += dot(xg_ref[:, 512:], kv_other[...].reshape(512, 256))
        lead_ref[8 : 8 + SEQ] = kv[:, :128]
        lead_ref[8 + SEQ :] = kv[:, 128:]

    q = dot(xg_ref[:, :512], own[...].reshape(512, 512))
    q += dot(xg_ref[:, 512:], other[...].reshape(512, 512))
    for h in range(4):
        out_ref[h] = jnp.concatenate(
            [lead_ref[...], q[:, HEAD * h : HEAD * h + HEAD]], axis=0
        ).astype(bf16)


def project(layer, scalars, xs, gains, weights, pieces):
    return pl.pallas_call(
        functools.partial(project_kernel, layer),
        grid=(4,),
        in_specs=[SMEM]
        + [whole(SEQ, COLS)] * 4
        + [pl.BlockSpec((64, 1024), lambda s: (0, s))] * 4
        + [whole(4, 4, COLS)]
        + [pl.BlockSpec((4, 128, 512), lambda s: (0, 0, s))] * 2
        + [pl.BlockSpec((4, 128, 256), lambda s: (0, 0, 8))] * 2,
        out_specs=[
            pl.BlockSpec((4, ROWS, 128), lambda s: (s, 0, 0)),
            pl.BlockSpec((4, 64, 1024), lambda s: (0, 0, s)),
        ],
        out_shape=[
            jax.ShapeDtypeStruct((16, ROWS, 128), bf16),
            jax.ShapeDtypeStruct((4, 64, OCOLS), bf16),
        ],
        scratch_shapes=[pltpu.VMEM((SEQ, 1024), bf16), pltpu.VMEM((8 + 2 * SEQ, 128), f32)],
        compiler_params=PARAMS,
        cost_estimate=cost(2 * SEQ * 1024 * SLAB, 6_000_000),
        name="project",
    )(scalars, *xs, *pieces, gains, *weights, *weights)


def attend_kernel(recv_ref, out_ref, acc):
    step = pl.program_id(0)

    @pl.when(step == 0)
    def _():
        acc[...] = jnp.sum(recv_ref[...].astype(f32), axis=0)

    @pl.when(step > 0)
    def _():
        acc[...] += jnp.sum(recv_ref[...].astype(f32), axis=0)

    @pl.when(step == 3)
    def _():
        row = lax.rsqrt((acc[0:1] + acc[1:2]) * (1.0 / WIDTH) + 1e-05)
        eye, _ = masks()
        column = jnp.sum(jnp.where(eye, row, 0.0), axis=1, keepdims=True)
        keys, values, queries = (
            (acc[8 + SEQ * k : 8 + SEQ * k + SEQ] * column).astype(bf16) for k in range(3)
        )
        scores = dot(queries, keys, ((1,), (1,))) * (1.0 / math.sqrt(HEAD))
        causal = lax.broadcasted_iota(jnp.int32, (SEQ, SEQ), 0) >= lax.broadcasted_iota(
            jnp.int32, (SEQ, SEQ), 1
        )
        weights = jnp.where(causal, jnp.exp(scores), 0.0)
        shares = (weights / jnp.sum(weights, axis=1, keepdims=True)).astype(bf16)
        out_ref[...] = dot(shares, values).astype(bf16)


def attend(received):
    return pl.pallas_call(
        attend_kernel,
        grid=(4,),
        in_specs=[pl.BlockSpec((4, ROWS, 128), lambda s: (s, 0, 0))],
        out_specs=whole(SEQ, HEAD),
        out_shape=jax.ShapeDtypeStruct((SEQ, HEAD), bf16),
        scratch_shapes=[pltpu.VMEM((ROWS, 128), f32)],
        compiler_params=PARAMS,
        cost_estimate=cost(6_000_000, 1_200_000),
        name="attend",
    )(received)


def output_kernel(scalars, *refs):
    mixed, own, other, mixed_ref = refs[:4], refs[4], refs[5], refs[-1]
    if len(refs) == 8:
        out_ref = refs[6]
    else:
        pieces, out_ref, joined_ref = refs[6:10], refs[10], refs[11]
        for k in range(4):
            joined_ref[k] = pieces[k][...]

    @pl.when(pl.program_id(0) == 0)
    def _():
        parts = [part[...].astype(f32) for part in mixed]
        low, high = [part[:, :64] for part in parts], [part[:, 64:] for part in parts]
        mixed_ref[...] = jnp.where(
            scalars[2] == 1, jnp.concatenate(high + low, axis=1), jnp.concatenate(low + high, axis=1)
        ).astype(bf16)

    o = dot(mixed_ref[:, :256], own[...].reshape(256, 1024))
    o += dot(mixed_ref[:, 256:], other[...].reshape(256, 1024))
    for i in range(4):
        out_ref[i] = o[:, COLS * i : COLS * i + COLS].astype(bf16)


def output(scalars, mixed, weights, pieces):
    specs = [SMEM] + [whole(SEQ, HEAD)] * 4 + [pl.BlockSpec((4, 64, 1024), lambda s: (0, 0, s))] * 2
    outs = [pltpu.HBM((16, SEQ, COLS), bf16)]
    out_specs = [pl.BlockSpec((4, SEQ, COLS), lambda s: (s, 0, 0))]
    if pieces:
        specs += [pl.BlockSpec((32, SLAB), lambda s: (s, 0))] * 4
        outs.append(pltpu.HBM((4, 128, SLAB), bf16))
        out_specs.append(pl.BlockSpec((4, 32, SLAB), lambda s: (0, s, 0)))
    return pl.pallas_call(
        output_kernel,
        grid=(4,),
        in_specs=specs,
        out_specs=out_specs,
        out_shape=outs,
        scratch_shapes=[pltpu.VMEM((SEQ, 512), bf16)],
        compiler_params=PARAMS,
        cost_estimate=cost(2 * SEQ * 512 * OCOLS, 10_000_000),
        name="output",
    )(scalars, *mixed, *weights, *pieces)


def close_kernel(recv_ref, x_ref, out_ref):
    out_ref[...] = (x_ref[...].astype(f32) + jnp.sum(recv_ref[...].astype(f32), axis=0)).astype(bf16)


def close(received, x):
    return pl.pallas_call(
        close_kernel,
        grid=(1,),
        in_specs=[whole(16, SEQ, COLS), whole(SEQ, COLS)],
        out_specs=whole(SEQ, COLS),
        out_shape=jax.ShapeDtypeStruct((SEQ, COLS), bf16),
        compiler_params=PARAMS,
        cost_estimate=cost(400_000, 800_000),
        name="close",
    )(received, x)


def exchange(value, axes):
    return lax.all_to_all(value, axes, 0, 0, tiled=True)


def across_line(value, axis, by):
    return lax.ppermute(value, axis, [(i, i ^ by) for i in range(4)])


def line(value, axis):
    near, far = (across_line(value, axis, by) for by in (1, 2))
    return [value, near, far, across_line(near, axis, 2)]


def after(gate, values):
    return lax.optimization_barrier((gate, values))


def relay(slabs, axis):
    near = [across_line(slabs[k], axis, k) for k in (1, 3)]
    near, far = after(near, slabs[2])
    return [slabs[0], near[0], across_line(far, axis, 2), near[1]]


def swapped(joined):
    return joined, lax.ppermute(joined, "c", [(0, 1), (1, 0)])


def body(entering, norm_gain, query_weight, key_matrix, value_matrix, output_weight):
    plane, across, along, core = (lax.axis_index(name) for name in ALL)
    slot = 2 * core + lax.rem(along, 2)
    scalars = jnp.stack([plane, along, core]).astype(jnp.int32)

    inward = lambda layer: slab_in(layer, scalars, query_weight, key_matrix, value_matrix)

    rounds = []
    for r in range(4):
        pairs = []
        for p in range(4):
            for t in range(32):
                s = (t // 8 - r) % 4
                pairs.append((32 * p + t, 32 * p + 2 * ((2 * t) % 16 + s % 2) + s // 2))
        s = lax.rem(across - r + 4, 4)
        piece = lax.dynamic_slice(entering, (s // 2, 0, lax.rem(s, 2) * COLS), (1, SEQ, COLS))[0]
        gain = lax.dynamic_slice(norm_gain, (0, lax.rem(s, 2) * COLS), (1, COLS))
        piece = jnp.concatenate([piece, jnp.broadcast_to(gain, (8, COLS))], axis=0)
        rounds.append(lax.ppermute(piece, ALL, pairs))
    rounds, (slab, cut) = after(rounds, (inward(0), slab_out(0, scalars, output_weight)))
    ins = relay(slab, "z")
    outs = relay(cut, "y")
    rounds = jnp.stack(rounds)
    xs = [
        lax.dynamic_index_in_dim(
            rounds, lax.rem(lax.bitwise_xor(plane, k) - slot + 4, 4), 0, keepdims=False
        )[:SEQ]
        for k in range(4)
    ]
    gains = jnp.stack(
        [
            lax.dynamic_index_in_dim(rounds[:, SEQ], lax.rem(p - slot + 4, 4), 0, keepdims=False)
            for p in range(4)
        ]
    )
    ahead = inward(1)
    ins, (outs, ahead, xs, gains) = after(ins, (outs, ahead, xs, gains))
    ins = swapped(join(ins))
    gains = jnp.stack(line(gains, "z")).astype(f32)
    states = []
    for layer in range(4):
        xs, outs = after(xs, outs)
        if layer < 3:
            xs, slab = after(xs, ahead)
            ins_next = relay(slab, "z")
        partial, outs = project(layer, scalars, xs, gains, ins, outs)
        if layer < 3:
            ins = ins_next
            partial, scalars = after(partial, scalars)
            cut = slab_out(layer + 1, scalars, output_weight)
            if layer < 2:
                ahead = inward(layer + 2)
        received, outs = after(exchange(partial, ("x", "y")), swapped(outs))
        if layer < 3:
            received, (cut, ahead) = after(received, (cut, ahead))
        mixed = line(attend(received), "y")
        if layer < 3:
            mixed, (ins, cut) = after(mixed, (ins, cut))
            outs_next = relay(cut, "y")
            partial, ins = output(scalars, mixed, outs, ins)
            ins = swapped(ins)
            outs = outs_next
        else:
            partial = output(scalars, mixed, outs, [])[0]
        x = close(exchange(partial, ("z", "x")), xs[0])
        states.append(x)
        if layer < 3:
            xs = line(x, "z")

    states = jnp.stack(states)
    rounds = []
    for k in range(4):
        pairs = [
            (2 * i + c, 32 * ((2 * c + i % 2 + k) % 4) + i // 2) for i in range(64) for c in range(2)
        ]
        piece = lax.dynamic_index_in_dim(states, lax.rem(slot + k, 4), 0, keepdims=False)
        rounds.append(lax.ppermute(piece, ALL, pairs))
    rounds = jnp.stack(rounds)
    pieces = [
        lax.dynamic_index_in_dim(rounds, lax.rem(plane - s + 4, 4), 0, keepdims=False) for s in range(4)
    ]
    return jnp.stack(
        [jnp.concatenate(pieces[:2], axis=1), jnp.concatenate(pieces[2:], axis=1)]
    )[None]


def solution(mesh):
    fine = Mesh(mesh.devices.reshape(4, 4, 4, 2), ALL)
    tp = ("x", "y", "c")
    rows = P(None, ALL, None)
    return jax.shard_map(
        body,
        mesh=fine,
        in_specs=(P(None, None, tp), P("z", tp), rows, rows, rows, rows),
        out_specs=P("z", None, None, tp),
        check_vma=False,
    )
```

```python
import functools
import math

import jax
import jax.numpy as jnp
from jax import lax
from jax.experimental import pallas as pl
from jax.experimental.pallas import tpu as pltpu
from jax.sharding import Mesh, PartitionSpec as P


ALL = ("z", "x", "y", "c")
HEAD = 128
SEQ = 88
COLS = 256
WIDTH = 16384
SLAB = 2304
OCOLS = 4096
ROWS = 272
VMEM_LIMIT = 52 * 1024 * 1024
f32 = jnp.float32
bf16 = jnp.bfloat16
SMEM = pl.BlockSpec(memory_space=pltpu.SMEM)
PARAMS = pltpu.CompilerParams(vmem_limit_bytes=VMEM_LIMIT)


def dot(a, b, contract=((1,), (0,))):
    return lax.dot_general(a, b, (contract, ((), ())), preferred_element_type=f32)


def whole(*shape):
    return pl.BlockSpec(shape, lambda s: (0,) * len(shape))


def cost(flops, size):
    return pl.CostEstimate(flops=flops, bytes_accessed=size, transcendentals=0)


def masks():
    rows = lax.broadcasted_iota(jnp.int32, (SEQ, 128), 0)
    lanes = lax.broadcasted_iota(jnp.int32, (SEQ, 128), 1)
    return rows == lanes, lanes <= rows


def slab_in_kernel(scalars, q_ref, k_ref, v_ref, *outs):
    for k, out in enumerate(outs):
        at = lax.bitwise_xor(scalars[0], k)
        out[:, :2048] = q_ref[0, :, pl.ds(pl.multiple_of(at * 2048, 2048), 2048)]
        out[:, 2048:2176] = k_ref[0, :, pl.ds(pl.multiple_of(at * 128, 128), 128)]
        out[:, 2176:] = v_ref[0, :, pl.ds(pl.multiple_of(at * 128, 128), 128)]


def slab_in(layer, scalars, q, k, v):
    return pl.pallas_call(
        slab_in_kernel,
        grid=(2,),
        in_specs=[
            SMEM,
            pl.BlockSpec((1, 64, 8192), lambda s: (layer, s, 0)),
            pl.BlockSpec((1, 64, 512), lambda s: (layer, s, 0)),
            pl.BlockSpec((1, 64, 512), lambda s: (layer, s, 0)),
        ],
        out_specs=[pl.BlockSpec((64, SLAB), lambda s: (s, 0))] * 4,
        out_shape=[pltpu.HBM((128, SLAB), bf16)] * 4,
        compiler_params=PARAMS,
        cost_estimate=cost(0, 4_700_000),
        name="slab_in",
    )(scalars, q, k, v)


def slab_out_kernel(scalars, o_ref, *outs):
    for k, out in enumerate(outs):
        at = lax.bitwise_xor(scalars[1], k) * COLS
        for s in range(16):
            out[:, COLS * s : COLS * s + COLS] = o_ref[
                0, :, pl.ds(pl.multiple_of(at + 1024 * s, COLS), COLS)
            ]


def slab_out(layer, scalars, o):
    return pl.pallas_call(
        slab_out_kernel,
        grid=(2,),
        in_specs=[SMEM, pl.BlockSpec((1, 32, WIDTH), lambda s: (layer, s, 0))],
        out_specs=[pl.BlockSpec((32, OCOLS), lambda s: (s, 0))] * 4,
        out_shape=[pltpu.HBM((64, OCOLS), bf16)] * 4,
        compiler_params=PARAMS,
        cost_estimate=cost(0, 4_200_000),
        name="slab_out",
    )(scalars, o)


def join_kernel(*refs):
    for k, ref in enumerate(refs[:4]):
        refs[4][k] = ref[...]


def join(pieces):
    rows, columns = pieces[0].shape
    half = rows // 2
    return pl.pallas_call(
        join_kernel,
        grid=(2,),
        in_specs=[pl.BlockSpec((half, columns), lambda s: (s, 0))] * 4,
        out_specs=pl.BlockSpec((4, half, columns), lambda s: (0, s, 0)),
        out_shape=pltpu.HBM((4, rows, columns), bf16),
        compiler_params=PARAMS,
        cost_estimate=cost(0, 4_500_000),
        name="join",
    )(*pieces)


def project_kernel(layer, scalars, *refs):
    xs, (gain_ref, own, other, kv_own, kv_other), refs = refs[:4], refs[4:9], refs[9:]
    if len(refs) == 8:
        pieces, out_ref, joined_ref = refs[:4], refs[4], refs[5]
        for k in range(4):
            joined_ref[k] = pieces[k][...]
    else:
        out_ref = refs[0]
    xg_ref, lead_ref = refs[-2:]
    z, core = scalars[0], scalars[2]

    @pl.when(pl.program_id(0) == 0)
    def _():
        rows = lax.broadcasted_iota(jnp.int32, (4, COLS), 0)
        gains = gain_ref[lax.bitwise_xor(z, layer)]
        total = jnp.zeros((SEQ, 1), f32)
        low, high = [], []
        for k in range(4):
            wide = xs[k][...].astype(f32)
            total += jnp.sum(wide * wide, axis=1, keepdims=True)
            at = rows == lax.bitwise_xor(z, k)
            scaled = wide * jnp.sum(jnp.where(at, gains, 0.0), axis=0, keepdims=True)
            low.append(scaled[:, :128])
            high.append(scaled[:, 128:])
        xg_ref[...] = jnp.where(
            core == 1, jnp.concatenate(high + low, axis=1), jnp.concatenate(low + high, axis=1)
        ).astype(bf16)
        eye, _ = masks()
        row = jnp.sum(jnp.where(eye, total, 0.0), axis=0, keepdims=True)
        coarse = row.astype(bf16).astype(f32)
        which = lax.broadcasted_iota(jnp.int32, (8, 128), 0)
        lead_ref[:8] = jnp.where(which == 0, coarse, jnp.where(which == 1, row - coarse, 0.0))
        kv = dot(xg_ref[:, :512], kv_own[...].reshape(512, 256))
        kv += dot(xg_ref[:, 512:], kv_other[...].reshape(512, 256))
        lead_ref[8 : 8 + SEQ] = kv[:, :128]
        lead_ref[8 + SEQ :] = kv[:, 128:]

    q = dot(xg_ref[:, :512], own[...].reshape(512, 512))
    q += dot(xg_ref[:, 512:], other[...].reshape(512, 512))
    for h in range(4):
        out_ref[h] = jnp.concatenate(
            [lead_ref[...], q[:, HEAD * h : HEAD * h + HEAD]], axis=0
        ).astype(bf16)


def project(layer, scalars, xs, gains, weights, pieces):
    specs = [SMEM] + [whole(SEQ, COLS)] * 4 + [whole(4, 4, COLS)]
    specs += [pl.BlockSpec((4, 128, 512), lambda s: (0, 0, s))] * 2
    specs += [pl.BlockSpec((4, 128, 256), lambda s: (0, 0, 8))] * 2
    outs = [pltpu.HBM((16, ROWS, 128), bf16)]
    out_specs = [pl.BlockSpec((4, ROWS, 128), lambda s: (s, 0, 0))]
    if pieces:
        specs += [pl.BlockSpec((64, 1024), lambda s: (0, s))] * 4
        outs.append(pltpu.HBM((4, 64, OCOLS), bf16))
        out_specs.append(pl.BlockSpec((4, 64, 1024), lambda s: (0, 0, s)))
    return pl.pallas_call(
        functools.partial(project_kernel, layer),
        grid=(4,),
        in_specs=specs,
        out_specs=out_specs,
        out_shape=outs,
        scratch_shapes=[pltpu.VMEM((SEQ, 1024), bf16), pltpu.VMEM((8 + 2 * SEQ, 128), f32)],
        compiler_params=PARAMS,
        cost_estimate=cost(2 * SEQ * 1024 * SLAB, 10_000_000),
        name="project",
    )(scalars, *xs, gains, *weights, *weights, *pieces)


def attend_kernel(recv_ref, out_ref, acc):
    step = pl.program_id(0)

    @pl.when(step == 0)
    def _():
        acc[...] = jnp.sum(recv_ref[...].astype(f32), axis=0)

    @pl.when(step > 0)
    def _():
        acc[...] += jnp.sum(recv_ref[...].astype(f32), axis=0)

    @pl.when(step == 3)
    def _():
        row = lax.rsqrt((acc[0:1] + acc[1:2]) * (1.0 / WIDTH) + 1e-05)
        eye, _ = masks()
        column = jnp.sum(jnp.where(eye, row, 0.0), axis=1, keepdims=True)
        keys, values, queries = (
            (acc[8 + SEQ * k : 8 + SEQ * k + SEQ] * column).astype(bf16) for k in range(3)
        )
        scores = dot(queries, keys, ((1,), (1,))) * (1.0 / math.sqrt(HEAD))
        causal = lax.broadcasted_iota(jnp.int32, (SEQ, SEQ), 0) >= lax.broadcasted_iota(
            jnp.int32, (SEQ, SEQ), 1
        )
        weights = jnp.where(causal, jnp.exp(scores), 0.0)
        shares = (weights / jnp.sum(weights, axis=1, keepdims=True)).astype(bf16)
        out_ref[...] = dot(shares, values).astype(bf16)


def attend(received):
    return pl.pallas_call(
        attend_kernel,
        grid=(4,),
        in_specs=[pl.BlockSpec((4, ROWS, 128), lambda s: (s, 0, 0))],
        out_specs=whole(SEQ, HEAD),
        out_shape=jax.ShapeDtypeStruct((SEQ, HEAD), bf16),
        scratch_shapes=[pltpu.VMEM((ROWS, 128), f32)],
        compiler_params=PARAMS,
        cost_estimate=cost(6_000_000, 1_200_000),
        name="attend",
    )(received)


def output_kernel(scalars, *refs):
    mixed, own, other, mixed_ref = refs[:4], refs[4], refs[5], refs[-1]
    if len(refs) == 8:
        out_ref = refs[6]
    else:
        pieces, out_ref, joined_ref = refs[6:10], refs[10], refs[11]
        for k in range(4):
            joined_ref[k] = pieces[k][...]

    @pl.when(pl.program_id(0) == 0)
    def _():
        parts = [part[...].astype(f32) for part in mixed]
        low, high = [part[:, :64] for part in parts], [part[:, 64:] for part in parts]
        mixed_ref[...] = jnp.where(
            scalars[2] == 1, jnp.concatenate(high + low, axis=1), jnp.concatenate(low + high, axis=1)
        ).astype(bf16)

    o = dot(mixed_ref[:, :256], own[...].reshape(256, 1024))
    o += dot(mixed_ref[:, 256:], other[...].reshape(256, 1024))
    for i in range(4):
        out_ref[i] = o[:, COLS * i : COLS * i + COLS].astype(bf16)


def output(scalars, mixed, weights, pieces):
    specs = [SMEM] + [whole(SEQ, HEAD)] * 4 + [pl.BlockSpec((4, 64, 1024), lambda s: (0, 0, s))] * 2
    outs = [pltpu.HBM((16, SEQ, COLS), bf16)]
    out_specs = [pl.BlockSpec((4, SEQ, COLS), lambda s: (s, 0, 0))]
    if pieces:
        specs += [pl.BlockSpec((32, SLAB), lambda s: (s, 0))] * 4
        outs.append(pltpu.HBM((4, 128, SLAB), bf16))
        out_specs.append(pl.BlockSpec((4, 32, SLAB), lambda s: (0, s, 0)))
    return pl.pallas_call(
        output_kernel,
        grid=(4,),
        in_specs=specs,
        out_specs=out_specs,
        out_shape=outs,
        scratch_shapes=[pltpu.VMEM((SEQ, 512), bf16)],
        compiler_params=PARAMS,
        cost_estimate=cost(2 * SEQ * 512 * OCOLS, 10_000_000),
        name="output",
    )(scalars, *mixed, *weights, *pieces)


def close_kernel(recv_ref, x_ref, out_ref):
    out_ref[...] = (x_ref[...].astype(f32) + jnp.sum(recv_ref[...].astype(f32), axis=0)).astype(bf16)


def close(received, x):
    return pl.pallas_call(
        close_kernel,
        grid=(1,),
        in_specs=[whole(16, SEQ, COLS), whole(SEQ, COLS)],
        out_specs=whole(SEQ, COLS),
        out_shape=jax.ShapeDtypeStruct((SEQ, COLS), bf16),
        compiler_params=PARAMS,
        cost_estimate=cost(400_000, 800_000),
        name="close",
    )(received, x)


def exchange(value, axes):
    return lax.all_to_all(value, axes, 0, 0, tiled=True)


def across_line(value, axis, by):
    return lax.ppermute(value, axis, [(i, i ^ by) for i in range(4)])


def line(value, axis):
    return [value] + [across_line(value, axis, k) for k in range(1, 4)]


def after(gate, values):
    return lax.optimization_barrier((gate, values))


def relay(slabs, axis):
    near = [across_line(slabs[k], axis, k) for k in (1, 3)]
    near, far = after(near, slabs[2])
    return [slabs[0], near[0], across_line(far, axis, 2), near[1]]


def swapped(joined):
    return joined, lax.ppermute(joined, "c", [(0, 1), (1, 0)])


def body(entering, norm_gain, query_weight, key_matrix, value_matrix, output_weight):
    plane, across, along, core = (lax.axis_index(name) for name in ALL)
    slot = 2 * core + lax.rem(along, 2)
    scalars = jnp.stack([plane, along, core]).astype(jnp.int32)

    inward = lambda layer: slab_in(layer, scalars, query_weight, key_matrix, value_matrix)

    rounds = []
    for r in range(4):
        pairs = []
        for p in range(4):
            for t in range(32):
                s = (t // 8 - r) % 4
                pairs.append((32 * p + t, 32 * p + 2 * ((2 * t) % 16 + s % 2) + s // 2))
        s = lax.rem(across - r + 4, 4)
        piece = lax.dynamic_slice(entering, (s // 2, 0, lax.rem(s, 2) * COLS), (1, SEQ, COLS))[0]
        gain = lax.dynamic_slice(norm_gain, (0, lax.rem(s, 2) * COLS), (1, COLS))
        piece = jnp.concatenate([piece, jnp.broadcast_to(gain, (8, COLS))], axis=0)
        rounds.append(lax.ppermute(piece, ALL, pairs))
    slab, cut = inward(0), slab_out(0, scalars, output_weight)
    near = [across_line(slab[k], "z", k) for k in (1, 3)]
    rounds, (near, far, cut) = after(rounds, (near, slab[2], cut))
    ins = [slab[0], near[0], across_line(far, "z", 2), near[1]]
    near = [across_line(cut[k], "y", k) for k in (1, 3)]
    rounds = jnp.stack(rounds)
    xs = [
        lax.dynamic_index_in_dim(
            rounds, lax.rem(lax.bitwise_xor(plane, k) - slot + 4, 4), 0, keepdims=False
        )[:SEQ]
        for k in range(4)
    ]
    gains = jnp.stack(
        [
            lax.dynamic_index_in_dim(rounds[:, SEQ], lax.rem(p - slot + 4, 4), 0, keepdims=False)
            for p in range(4)
        ]
    )
    ahead = inward(1)
    ins, (near, far, ahead, xs, gains) = after(ins, (near, cut[2], ahead, xs, gains))
    outs = [cut[0], near[0], across_line(far, "y", 2), near[1]]
    ins = swapped(join(ins))
    gains = jnp.stack(line(gains, "z")).astype(f32)
    states = []
    for layer in range(4):
        if layer:
            xs, outs = after(xs, outs)
        if layer < 3:
            xs, slab = after(xs, ahead)
            ins_next = relay(slab, "z")
        if layer:
            partial, outs = project(layer, scalars, xs, gains, ins, outs)
        else:
            partial = project(layer, scalars, xs, gains, ins, [])[0]
            partial, outs = after(partial, outs)
            outs = join(outs)
        if layer < 3:
            ins = ins_next
            partial, scalars = after(partial, scalars)
            cut = slab_out(layer + 1, scalars, output_weight)
            if layer < 2:
                ahead = inward(layer + 2)
        received, outs = after(exchange(partial, ("x", "y")), swapped(outs))
        if layer < 3:
            received, (cut, ahead) = after(received, (cut, ahead))
        mixed = line(attend(received), "y")
        if layer < 3:
            mixed, (ins, cut) = after(mixed, (ins, cut))
            outs_next = relay(cut, "y")
            partial, ins = output(scalars, mixed, outs, ins)
            ins = swapped(ins)
            outs = outs_next
        else:
            partial = output(scalars, mixed, outs, [])[0]
        x = close(exchange(partial, ("z", "x")), xs[0])
        states.append(x)
        if layer < 3:
            xs = line(x, "z")

    states = jnp.stack(states)
    rounds = []
    for k in range(4):
        pairs = [
            (2 * i + c, 32 * ((2 * c + i % 2 + k) % 4) + i // 2) for i in range(64) for c in range(2)
        ]
        piece = lax.dynamic_index_in_dim(states, lax.rem(slot + k, 4), 0, keepdims=False)
        rounds.append(lax.ppermute(piece, ALL, pairs))
    rounds = jnp.stack(rounds)
    pieces = [
        lax.dynamic_index_in_dim(rounds, lax.rem(plane - s + 4, 4), 0, keepdims=False) for s in range(4)
    ]
    return jnp.stack(
        [jnp.concatenate(pieces[:2], axis=1), jnp.concatenate(pieces[2:], axis=1)]
    )[None]


def solution(mesh):
    fine = Mesh(mesh.devices.reshape(4, 4, 4, 2), ALL)
    tp = ("x", "y", "c")
    rows = P(None, ALL, None)
    return jax.shard_map(
        body,
        mesh=fine,
        in_specs=(P(None, None, tp), P("z", tp), rows, rows, rows, rows),
        out_specs=P("z", None, None, tp),
        check_vma=False,
    )
```

```python
import functools
import math

import jax
import jax.numpy as jnp
from jax import lax
from jax.experimental import pallas as pl
from jax.experimental.pallas import tpu as pltpu
from jax.sharding import Mesh, PartitionSpec as P


ALL = ("z", "x", "y", "c")
HEAD = 128
SEQ = 88
COLS = 256
WIDTH = 16384
SLAB = 2304
OCOLS = 4096
ROWS = 272
VMEM_LIMIT = 52 * 1024 * 1024
f32 = jnp.float32
bf16 = jnp.bfloat16
SMEM = pl.BlockSpec(memory_space=pltpu.SMEM)
PARAMS = pltpu.CompilerParams(vmem_limit_bytes=VMEM_LIMIT)


def dot(a, b, contract=((1,), (0,))):
    return lax.dot_general(a, b, (contract, ((), ())), preferred_element_type=f32)


def whole(*shape):
    return pl.BlockSpec(shape, lambda s: (0,) * len(shape))


def cost(flops, size):
    return pl.CostEstimate(flops=flops, bytes_accessed=size, transcendentals=0)


def masks():
    rows = lax.broadcasted_iota(jnp.int32, (SEQ, 128), 0)
    lanes = lax.broadcasted_iota(jnp.int32, (SEQ, 128), 1)
    return rows == lanes, lanes <= rows


def slab_in_kernel(scalars, q_ref, k_ref, v_ref, *outs):
    for k, out in enumerate(outs):
        at = lax.bitwise_xor(scalars[0], k)
        out[:, :2048] = q_ref[0, :, pl.ds(pl.multiple_of(at * 2048, 2048), 2048)]
        out[:, 2048:2176] = k_ref[0, :, pl.ds(pl.multiple_of(at * 128, 128), 128)]
        out[:, 2176:] = v_ref[0, :, pl.ds(pl.multiple_of(at * 128, 128), 128)]


def slab_in(layer, scalars, q, k, v):
    return pl.pallas_call(
        slab_in_kernel,
        grid=(2,),
        in_specs=[
            SMEM,
            pl.BlockSpec((1, 64, 8192), lambda s: (layer, s, 0)),
            pl.BlockSpec((1, 64, 512), lambda s: (layer, s, 0)),
            pl.BlockSpec((1, 64, 512), lambda s: (layer, s, 0)),
        ],
        out_specs=[pl.BlockSpec((64, SLAB), lambda s: (s, 0))] * 4,
        out_shape=[pltpu.HBM((128, SLAB), bf16)] * 4,
        compiler_params=PARAMS if layer else pltpu.CompilerParams(vmem_limit_bytes=62 * 1024 * 1024),
        cost_estimate=cost(0, 4_700_000),
        name="slab_in",
    )(scalars, q, k, v)


def slab_out_kernel(scalars, o_ref, *outs):
    for k, out in enumerate(outs):
        at = lax.bitwise_xor(scalars[1], k) * COLS
        for s in range(16):
            out[:, COLS * s : COLS * s + COLS] = o_ref[
                0, :, pl.ds(pl.multiple_of(at + 1024 * s, COLS), COLS)
            ]


def slab_out(layer, scalars, o):
    return pl.pallas_call(
        slab_out_kernel,
        grid=(2,),
        in_specs=[SMEM, pl.BlockSpec((1, 32, WIDTH), lambda s: (layer, s, 0))],
        out_specs=[pl.BlockSpec((32, OCOLS), lambda s: (s, 0))] * 4,
        out_shape=[pltpu.HBM((64, OCOLS), bf16)] * 4,
        compiler_params=PARAMS,
        cost_estimate=cost(0, 4_200_000),
        name="slab_out",
    )(scalars, o)


def join_kernel(*refs):
    for k, ref in enumerate(refs[:4]):
        refs[4][k] = ref[...]


def join(pieces):
    rows, columns = pieces[0].shape
    half = rows // 2
    return pl.pallas_call(
        join_kernel,
        grid=(2,),
        in_specs=[pl.BlockSpec((half, columns), lambda s: (s, 0))] * 4,
        out_specs=pl.BlockSpec((4, half, columns), lambda s: (0, s, 0)),
        out_shape=pltpu.HBM((4, rows, columns), bf16),
        compiler_params=PARAMS,
        cost_estimate=cost(0, 4_500_000),
        name="join",
    )(*pieces)


def project_kernel(layer, scalars, *refs):
    xs, (gain_ref, own, other, kv_own, kv_other), refs = refs[:4], refs[4:9], refs[9:]
    if len(refs) == 8:
        pieces, out_ref, joined_ref = refs[:4], refs[4], refs[5]
        for k in range(4):
            joined_ref[k] = pieces[k][...]
    else:
        out_ref = refs[0]
    xg_ref, lead_ref = refs[-2:]
    z, core = scalars[0], scalars[2]

    @pl.when(pl.program_id(0) == 0)
    def _():
        rows = lax.broadcasted_iota(jnp.int32, (4, COLS), 0)
        gains = gain_ref[lax.bitwise_xor(z, layer)]
        total = jnp.zeros((SEQ, 1), f32)
        low, high = [], []
        for k in range(4):
            wide = xs[k][...].astype(f32)
            total += jnp.sum(wide * wide, axis=1, keepdims=True)
            at = rows == lax.bitwise_xor(z, k)
            scaled = wide * jnp.sum(jnp.where(at, gains, 0.0), axis=0, keepdims=True)
            low.append(scaled[:, :128])
            high.append(scaled[:, 128:])
        xg_ref[...] = jnp.where(
            core == 1, jnp.concatenate(high + low, axis=1), jnp.concatenate(low + high, axis=1)
        ).astype(bf16)
        eye, _ = masks()
        row = jnp.sum(jnp.where(eye, total, 0.0), axis=0, keepdims=True)
        coarse = row.astype(bf16).astype(f32)
        which = lax.broadcasted_iota(jnp.int32, (8, 128), 0)
        lead_ref[:8] = jnp.where(which == 0, coarse, jnp.where(which == 1, row - coarse, 0.0))
        kv = dot(xg_ref[:, :512], kv_own[...].reshape(512, 256))
        kv += dot(xg_ref[:, 512:], kv_other[...].reshape(512, 256))
        lead_ref[8 : 8 + SEQ] = kv[:, :128]
        lead_ref[8 + SEQ :] = kv[:, 128:]

    q = dot(xg_ref[:, :512], own[...].reshape(512, 1024))
    q += dot(xg_ref[:, 512:], other[...].reshape(512, 1024))
    for h in range(8):
        out_ref[h] = jnp.concatenate(
            [lead_ref[...], q[:, HEAD * h : HEAD * h + HEAD]], axis=0
        ).astype(bf16)


def project(layer, scalars, xs, gains, weights, pieces):
    specs = [SMEM] + [whole(SEQ, COLS)] * 4 + [whole(4, 4, COLS)]
    specs += [pl.BlockSpec((4, 128, 1024), lambda s: (0, 0, s))] * 2
    specs += [pl.BlockSpec((4, 128, 256), lambda s: (0, 0, 8))] * 2
    outs = [pltpu.HBM((16, ROWS, 128), bf16)]
    out_specs = [pl.BlockSpec((8, ROWS, 128), lambda s: (s, 0, 0))]
    if pieces:
        specs += [pl.BlockSpec((64, 2048), lambda s: (0, s))] * 4
        outs.append(pltpu.HBM((4, 64, OCOLS), bf16))
        out_specs.append(pl.BlockSpec((4, 64, 2048), lambda s: (0, 0, s)))
    return pl.pallas_call(
        functools.partial(project_kernel, layer),
        grid=(2,),
        in_specs=specs,
        out_specs=out_specs,
        out_shape=outs,
        scratch_shapes=[pltpu.VMEM((SEQ, 1024), bf16), pltpu.VMEM((8 + 2 * SEQ, 128), f32)],
        compiler_params=PARAMS,
        cost_estimate=cost(2 * SEQ * 1024 * SLAB, 10_000_000),
        name="project",
    )(scalars, *xs, gains, *weights, *weights, *pieces)


def attend_kernel(recv_ref, out_ref, acc):
    step = pl.program_id(0)

    @pl.when(step == 0)
    def _():
        acc[...] = jnp.sum(recv_ref[...].astype(f32), axis=0)

    @pl.when(step > 0)
    def _():
        acc[...] += jnp.sum(recv_ref[...].astype(f32), axis=0)

    @pl.when(step == 3)
    def _():
        row = lax.rsqrt((acc[0:1] + acc[1:2]) * (1.0 / WIDTH) + 1e-05)
        eye, _ = masks()
        column = jnp.sum(jnp.where(eye, row, 0.0), axis=1, keepdims=True)
        keys, values, queries = (
            (acc[8 + SEQ * k : 8 + SEQ * k + SEQ] * column).astype(bf16) for k in range(3)
        )
        scores = dot(queries, keys, ((1,), (1,))) * (1.0 / math.sqrt(HEAD))
        causal = lax.broadcasted_iota(jnp.int32, (SEQ, SEQ), 0) >= lax.broadcasted_iota(
            jnp.int32, (SEQ, SEQ), 1
        )
        weights = jnp.where(causal, jnp.exp(scores), 0.0)
        shares = (weights / jnp.sum(weights, axis=1, keepdims=True)).astype(bf16)
        out_ref[...] = dot(shares, values).astype(bf16)


def attend(received):
    return pl.pallas_call(
        attend_kernel,
        grid=(4,),
        in_specs=[pl.BlockSpec((4, ROWS, 128), lambda s: (s, 0, 0))],
        out_specs=whole(SEQ, HEAD),
        out_shape=jax.ShapeDtypeStruct((SEQ, HEAD), bf16),
        scratch_shapes=[pltpu.VMEM((ROWS, 128), f32)],
        compiler_params=PARAMS,
        cost_estimate=cost(6_000_000, 1_200_000),
        name="attend",
    )(received)


def output_kernel(scalars, *refs):
    mixed, own, other, mixed_ref = refs[:4], refs[4], refs[5], refs[-1]
    if len(refs) == 8:
        out_ref = refs[6]
    else:
        pieces, out_ref, joined_ref = refs[6:10], refs[10], refs[11]
        for k in range(4):
            joined_ref[k] = pieces[k][...]

    @pl.when(pl.program_id(0) == 0)
    def _():
        parts = [part[...].astype(f32) for part in mixed]
        low, high = [part[:, :64] for part in parts], [part[:, 64:] for part in parts]
        mixed_ref[...] = jnp.where(
            scalars[2] == 1, jnp.concatenate(high + low, axis=1), jnp.concatenate(low + high, axis=1)
        ).astype(bf16)

    o = dot(mixed_ref[:, :256], own[...].reshape(256, 2048))
    o += dot(mixed_ref[:, 256:], other[...].reshape(256, 2048))
    for i in range(8):
        out_ref[i] = o[:, COLS * i : COLS * i + COLS].astype(bf16)


def output(scalars, mixed, weights, pieces):
    specs = [SMEM] + [whole(SEQ, HEAD)] * 4 + [pl.BlockSpec((4, 64, 2048), lambda s: (0, 0, s))] * 2
    outs = [pltpu.HBM((16, SEQ, COLS), bf16)]
    out_specs = [pl.BlockSpec((8, SEQ, COLS), lambda s: (s, 0, 0))]
    if pieces:
        specs += [pl.BlockSpec((64, SLAB), lambda s: (s, 0))] * 4
        outs.append(pltpu.HBM((4, 128, SLAB), bf16))
        out_specs.append(pl.BlockSpec((4, 64, SLAB), lambda s: (0, s, 0)))
    return pl.pallas_call(
        output_kernel,
        grid=(2,),
        in_specs=specs,
        out_specs=out_specs,
        out_shape=outs,
        scratch_shapes=[pltpu.VMEM((SEQ, 512), bf16)],
        compiler_params=PARAMS,
        cost_estimate=cost(2 * SEQ * 512 * OCOLS, 10_000_000),
        name="output",
    )(scalars, *mixed, *weights, *pieces)


def close_kernel(recv_ref, x_ref, out_ref):
    out_ref[...] = (x_ref[...].astype(f32) + jnp.sum(recv_ref[...].astype(f32), axis=0)).astype(bf16)


def close(received, x):
    return pl.pallas_call(
        close_kernel,
        grid=(1,),
        in_specs=[whole(16, SEQ, COLS), whole(SEQ, COLS)],
        out_specs=whole(SEQ, COLS),
        out_shape=jax.ShapeDtypeStruct((SEQ, COLS), bf16),
        compiler_params=PARAMS,
        cost_estimate=cost(400_000, 800_000),
        name="close",
    )(received, x)


def exchange(value, axes):
    return lax.all_to_all(value, axes, 0, 0, tiled=True)


def across_line(value, axis, by):
    return lax.ppermute(value, axis, [(i, i ^ by) for i in range(4)])


def line(value, axis):
    return [value] + [across_line(value, axis, k) for k in range(1, 4)]


def after(gate, values):
    return lax.optimization_barrier((gate, values))


def relay(slabs, axis):
    near = [across_line(slabs[k], axis, k) for k in (1, 3)]
    near, far = after(near, slabs[2])
    return [slabs[0], near[0], across_line(far, axis, 2), near[1]]


def swapped(joined):
    return joined, lax.ppermute(joined, "c", [(0, 1), (1, 0)])


def body(entering, norm_gain, query_weight, key_matrix, value_matrix, output_weight):
    plane, across, along, core = (lax.axis_index(name) for name in ALL)
    slot = 2 * core + lax.rem(along, 2)
    scalars = jnp.stack([plane, along, core]).astype(jnp.int32)

    inward = lambda layer: slab_in(layer, scalars, query_weight, key_matrix, value_matrix)

    rounds = []
    for r in range(4):
        pairs = []
        for p in range(4):
            for t in range(32):
                s = (t // 8 - r) % 4
                pairs.append((32 * p + t, 32 * p + 2 * ((2 * t) % 16 + s % 2) + s // 2))
        s = lax.rem(across - r + 4, 4)
        piece = lax.dynamic_slice(entering, (s // 2, 0, lax.rem(s, 2) * COLS), (1, SEQ, COLS))[0]
        gain = lax.dynamic_slice(norm_gain, (0, lax.rem(s, 2) * COLS), (1, COLS))
        piece = jnp.concatenate([piece, jnp.broadcast_to(gain, (8, COLS))], axis=0)
        rounds.append(lax.ppermute(piece, ALL, pairs))
    slab, cut = inward(0), slab_out(0, scalars, output_weight)
    near = [across_line(slab[k], "z", k) for k in (1, 3)]
    rounds, (near, far, cut) = after(rounds, (near, slab[2], cut))
    ins = [slab[0], near[0], across_line(far, "z", 2), near[1]]
    near = [across_line(cut[k], "y", k) for k in (1, 3)]
    rounds = jnp.stack(rounds)
    xs = [
        lax.dynamic_index_in_dim(
            rounds, lax.rem(lax.bitwise_xor(plane, k) - slot + 4, 4), 0, keepdims=False
        )[:SEQ]
        for k in range(4)
    ]
    gains = jnp.stack(
        [
            lax.dynamic_index_in_dim(rounds[:, SEQ], lax.rem(p - slot + 4, 4), 0, keepdims=False)
            for p in range(4)
        ]
    )
    ahead = inward(1)
    ins, (near, far, ahead, xs, gains) = after(ins, (near, cut[2], ahead, xs, gains))
    outs = [cut[0], near[0], across_line(far, "y", 2), near[1]]
    ins = swapped(join(ins))
    gains = jnp.stack(line(gains, "z")).astype(f32)
    states = []
    for layer in range(4):
        if layer:
            xs, outs = after(xs, outs)
        if layer < 3:
            xs, slab = after(xs, ahead)
            ins_next = relay(slab, "z")
        if layer:
            partial, outs = project(layer, scalars, xs, gains, ins, outs)
        else:
            partial = project(layer, scalars, xs, gains, ins, [])[0]
            partial, outs = after(partial, outs)
            outs = join(outs)
        if layer < 3:
            ins = ins_next
            partial, scalars = after(partial, scalars)
            cut = slab_out(layer + 1, scalars, output_weight)
            if layer < 2:
                ahead = inward(layer + 2)
        received, outs = after(exchange(partial, ("x", "y")), swapped(outs))
        if layer < 3:
            received, (cut, ahead) = after(received, (cut, ahead))
        mixed = line(attend(received), "y")
        if layer < 3:
            mixed, (ins, cut) = after(mixed, (ins, cut))
            outs_next = relay(cut, "y")
            partial, ins = output(scalars, mixed, outs, ins)
            ins = swapped(ins)
            outs = outs_next
        else:
            partial = output(scalars, mixed, outs, [])[0]
        x = close(exchange(partial, ("z", "x")), xs[0])
        states.append(x)
        if layer < 3:
            xs = line(x, "z")

    states = jnp.stack(states)
    rounds = []
    for k in range(4):
        pairs = [
            (2 * i + c, 32 * ((2 * c + i % 2 + k) % 4) + i // 2) for i in range(64) for c in range(2)
        ]
        piece = lax.dynamic_index_in_dim(states, lax.rem(slot + k, 4), 0, keepdims=False)
        rounds.append(lax.ppermute(piece, ALL, pairs))
    rounds = jnp.stack(rounds)
    pieces = [
        lax.dynamic_index_in_dim(rounds, lax.rem(plane - s + 4, 4), 0, keepdims=False) for s in range(4)
    ]
    return jnp.stack(
        [jnp.concatenate(pieces[:2], axis=1), jnp.concatenate(pieces[2:], axis=1)]
    )[None]


def solution(mesh):
    fine = Mesh(mesh.devices.reshape(4, 4, 4, 2), ALL)
    tp = ("x", "y", "c")
    rows = P(None, ALL, None)
    return jax.shard_map(
        body,
        mesh=fine,
        in_specs=(P(None, None, tp), P("z", tp), rows, rows, rows, rows),
        out_specs=P("z", None, None, tp),
        check_vma=False,
    )
```

```python
import functools
import math

import jax
import jax.numpy as jnp
from jax import lax
from jax.experimental import pallas as pl
from jax.experimental.pallas import tpu as pltpu
from jax.sharding import Mesh, PartitionSpec as P


ALL = ("z", "x", "y", "c")
HEAD = 128
SEQ = 88
COLS = 256
WIDTH = 16384
SLAB = 2304
OCOLS = 4096
ROWS = 272
VMEM_LIMIT = 52 * 1024 * 1024
f32 = jnp.float32
bf16 = jnp.bfloat16
SMEM = pl.BlockSpec(memory_space=pltpu.SMEM)
PARAMS = pltpu.CompilerParams(vmem_limit_bytes=VMEM_LIMIT)


def dot(a, b, contract=((1,), (0,))):
    return lax.dot_general(a, b, (contract, ((), ())), preferred_element_type=f32)


def whole(*shape):
    return pl.BlockSpec(shape, lambda s: (0,) * len(shape))


def cost(flops, size):
    return pl.CostEstimate(flops=flops, bytes_accessed=size, transcendentals=0)


def masks():
    rows = lax.broadcasted_iota(jnp.int32, (SEQ, 128), 0)
    lanes = lax.broadcasted_iota(jnp.int32, (SEQ, 128), 1)
    return rows == lanes, lanes <= rows


def slab_in_kernel(scalars, q_ref, k_ref, v_ref, *outs):
    for k, out in enumerate(outs):
        at = lax.bitwise_xor(scalars[0], k)
        out[:, :2048] = q_ref[0, :, pl.ds(pl.multiple_of(at * 2048, 2048), 2048)]
        out[:, 2048:2176] = k_ref[0, :, pl.ds(pl.multiple_of(at * 128, 128), 128)]
        out[:, 2176:] = v_ref[0, :, pl.ds(pl.multiple_of(at * 128, 128), 128)]


def slab_in(layer, scalars, q, k, v):
    return pl.pallas_call(
        slab_in_kernel,
        grid=(2,),
        in_specs=[
            SMEM,
            pl.BlockSpec((1, 64, 8192), lambda s: (layer, s, 0)),
            pl.BlockSpec((1, 64, 512), lambda s: (layer, s, 0)),
            pl.BlockSpec((1, 64, 512), lambda s: (layer, s, 0)),
        ],
        out_specs=[pl.BlockSpec((64, SLAB), lambda s: (s, 0))] * 4,
        out_shape=[pltpu.HBM((128, SLAB), bf16)] * 4,
        compiler_params=PARAMS if layer else pltpu.CompilerParams(vmem_limit_bytes=62 * 1024 * 1024),
        cost_estimate=cost(0, 4_700_000),
        name="slab_in",
    )(scalars, q, k, v)


def slab_out_kernel(scalars, o_ref, *outs):
    for k, out in enumerate(outs):
        at = lax.bitwise_xor(scalars[1], k) * COLS
        for s in range(16):
            out[:, COLS * s : COLS * s + COLS] = o_ref[
                0, :, pl.ds(pl.multiple_of(at + 1024 * s, COLS), COLS)
            ]


def slab_out(layer, scalars, o):
    return pl.pallas_call(
        slab_out_kernel,
        grid=(2,),
        in_specs=[SMEM, pl.BlockSpec((1, 32, WIDTH), lambda s: (layer, s, 0))],
        out_specs=[pl.BlockSpec((32, OCOLS), lambda s: (s, 0))] * 4,
        out_shape=[pltpu.HBM((64, OCOLS), bf16)] * 4,
        compiler_params=PARAMS,
        cost_estimate=cost(0, 4_200_000),
        name="slab_out",
    )(scalars, o)


def join_kernel(*refs):
    for k, ref in enumerate(refs[:4]):
        refs[4][k] = ref[...]


def join(pieces):
    rows, columns = pieces[0].shape
    half = rows // 2
    return pl.pallas_call(
        join_kernel,
        grid=(2,),
        in_specs=[pl.BlockSpec((half, columns), lambda s: (s, 0))] * 4,
        out_specs=pl.BlockSpec((4, half, columns), lambda s: (0, s, 0)),
        out_shape=pltpu.HBM((4, rows, columns), bf16),
        compiler_params=PARAMS,
        cost_estimate=cost(0, 4_500_000),
        name="join",
    )(*pieces)


def project_kernel(layer, scalars, *refs):
    xs, (gain_ref, own, other, kv_own, kv_other), refs = refs[:4], refs[4:9], refs[9:]
    if len(refs) == 8:
        pieces, out_ref, joined_ref = refs[:4], refs[4], refs[5]
        for k in range(4):
            joined_ref[k] = pieces[k][...]
    else:
        out_ref = refs[0]
    xg_ref, lead_ref = refs[-2:]
    z, core = scalars[0], scalars[2]

    @pl.when(pl.program_id(0) == 0)
    def _():
        rows = lax.broadcasted_iota(jnp.int32, (4, COLS), 0)
        gains = gain_ref[lax.bitwise_xor(z, layer)]
        total = jnp.zeros((SEQ, 1), f32)
        low, high = [], []
        for k in range(4):
            wide = xs[k][...].astype(f32)
            total += jnp.sum(wide * wide, axis=1, keepdims=True)
            at = rows == lax.bitwise_xor(z, k)
            scaled = wide * jnp.sum(jnp.where(at, gains, 0.0), axis=0, keepdims=True)
            low.append(scaled[:, :128])
            high.append(scaled[:, 128:])
        xg_ref[...] = jnp.where(
            core == 1, jnp.concatenate(high + low, axis=1), jnp.concatenate(low + high, axis=1)
        ).astype(bf16)
        eye, _ = masks()
        row = jnp.sum(jnp.where(eye, total, 0.0), axis=0, keepdims=True)
        coarse = row.astype(bf16).astype(f32)
        which = lax.broadcasted_iota(jnp.int32, (8, 128), 0)
        lead_ref[:8] = jnp.where(which == 0, coarse, jnp.where(which == 1, row - coarse, 0.0))
        kv = dot(xg_ref[:, :512], kv_own[...].reshape(512, 256))
        kv += dot(xg_ref[:, 512:], kv_other[...].reshape(512, 256))
        lead_ref[8 : 8 + SEQ] = kv[:, :128]
        lead_ref[8 + SEQ :] = kv[:, 128:]

    q = dot(xg_ref[:, :512], own[...].reshape(512, 1024))
    q += dot(xg_ref[:, 512:], other[...].reshape(512, 1024))
    for h in range(8):
        out_ref[h] = jnp.concatenate(
            [lead_ref[...], q[:, HEAD * h : HEAD * h + HEAD]], axis=0
        ).astype(bf16)


def project(layer, scalars, xs, gains, weights, pieces):
    specs = [SMEM] + [whole(SEQ, COLS)] * 4 + [whole(4, 4, COLS)]
    specs += [pl.BlockSpec((4, 128, 1024), lambda s: (0, 0, s))] * 2
    specs += [pl.BlockSpec((4, 128, 256), lambda s: (0, 0, 8))] * 2
    outs = [pltpu.HBM((16, ROWS, 128), bf16)]
    out_specs = [pl.BlockSpec((8, ROWS, 128), lambda s: (s, 0, 0))]
    if pieces:
        specs += [pl.BlockSpec((64, 2048), lambda s: (0, s))] * 4
        outs.append(pltpu.HBM((4, 64, OCOLS), bf16))
        out_specs.append(pl.BlockSpec((4, 64, 2048), lambda s: (0, 0, s)))
    return pl.pallas_call(
        functools.partial(project_kernel, layer),
        grid=(2,),
        in_specs=specs,
        out_specs=out_specs,
        out_shape=outs,
        scratch_shapes=[pltpu.VMEM((SEQ, 1024), bf16), pltpu.VMEM((8 + 2 * SEQ, 128), f32)],
        compiler_params=PARAMS,
        cost_estimate=cost(2 * SEQ * 1024 * SLAB, 10_000_000),
        name="project",
    )(scalars, *xs, gains, *weights, *weights, *pieces)


def attend_kernel(recv_ref, out_ref, acc):
    step = pl.program_id(0)

    @pl.when(step == 0)
    def _():
        acc[...] = jnp.sum(recv_ref[...].astype(f32), axis=0)

    @pl.when(step > 0)
    def _():
        acc[...] += jnp.sum(recv_ref[...].astype(f32), axis=0)

    @pl.when(step == 3)
    def _():
        row = lax.rsqrt((acc[0:1] + acc[1:2]) * (1.0 / WIDTH) + 1e-05)
        eye, _ = masks()
        column = jnp.sum(jnp.where(eye, row, 0.0), axis=1, keepdims=True)
        keys, values, queries = (
            (acc[8 + SEQ * k : 8 + SEQ * k + SEQ] * column).astype(bf16) for k in range(3)
        )
        scores = dot(queries, keys, ((1,), (1,))) * (1.0 / math.sqrt(HEAD))
        causal = lax.broadcasted_iota(jnp.int32, (SEQ, SEQ), 0) >= lax.broadcasted_iota(
            jnp.int32, (SEQ, SEQ), 1
        )
        weights = jnp.where(causal, jnp.exp(scores), 0.0)
        shares = (weights / jnp.sum(weights, axis=1, keepdims=True)).astype(bf16)
        out_ref[...] = dot(shares, values).astype(bf16)


def attend(received):
    return pl.pallas_call(
        attend_kernel,
        grid=(4,),
        in_specs=[pl.BlockSpec((4, ROWS, 128), lambda s: (s, 0, 0))],
        out_specs=whole(SEQ, HEAD),
        out_shape=jax.ShapeDtypeStruct((SEQ, HEAD), bf16),
        scratch_shapes=[pltpu.VMEM((ROWS, 128), f32)],
        compiler_params=PARAMS,
        cost_estimate=cost(6_000_000, 1_200_000),
        name="attend",
    )(received)


def output_kernel(scalars, *refs):
    mixed, own, other, mixed_ref = refs[:4], refs[4], refs[5], refs[-1]
    if len(refs) == 8:
        out_ref = refs[6]
    else:
        pieces, out_ref, joined_ref = refs[6:10], refs[10], refs[11]
        for k in range(4):
            joined_ref[k] = pieces[k][...]

    @pl.when(pl.program_id(0) == 0)
    def _():
        parts = [part[...].astype(f32) for part in mixed]
        low, high = [part[:, :64] for part in parts], [part[:, 64:] for part in parts]
        mixed_ref[...] = jnp.where(
            scalars[2] == 1, jnp.concatenate(high + low, axis=1), jnp.concatenate(low + high, axis=1)
        ).astype(bf16)

    o = dot(mixed_ref[:, :256], own[...].reshape(256, 2048))
    o += dot(mixed_ref[:, 256:], other[...].reshape(256, 2048))
    for i in range(8):
        out_ref[i] = o[:, COLS * i : COLS * i + COLS].astype(bf16)


def output(scalars, mixed, weights, pieces):
    specs = [SMEM] + [whole(SEQ, HEAD)] * 4 + [pl.BlockSpec((4, 64, 2048), lambda s: (0, 0, s))] * 2
    outs = [pltpu.HBM((16, SEQ, COLS), bf16)]
    out_specs = [pl.BlockSpec((8, SEQ, COLS), lambda s: (s, 0, 0))]
    if pieces:
        specs += [pl.BlockSpec((64, SLAB), lambda s: (s, 0))] * 4
        outs.append(pltpu.HBM((4, 128, SLAB), bf16))
        out_specs.append(pl.BlockSpec((4, 64, SLAB), lambda s: (0, s, 0)))
    return pl.pallas_call(
        output_kernel,
        grid=(2,),
        in_specs=specs,
        out_specs=out_specs,
        out_shape=outs,
        scratch_shapes=[pltpu.VMEM((SEQ, 512), bf16)],
        compiler_params=PARAMS,
        cost_estimate=cost(2 * SEQ * 512 * OCOLS, 10_000_000),
        name="output",
    )(scalars, *mixed, *weights, *pieces)


def close_kernel(recv_ref, x_ref, out_ref):
    out_ref[...] = (x_ref[...].astype(f32) + jnp.sum(recv_ref[...].astype(f32), axis=0)).astype(bf16)


def close(received, x):
    return pl.pallas_call(
        close_kernel,
        grid=(1,),
        in_specs=[whole(16, SEQ, COLS), whole(SEQ, COLS)],
        out_specs=whole(SEQ, COLS),
        out_shape=jax.ShapeDtypeStruct((SEQ, COLS), bf16),
        compiler_params=PARAMS,
        cost_estimate=cost(400_000, 800_000),
        name="close",
    )(received, x)


def exchange(value, axes):
    return lax.all_to_all(value, axes, 0, 0, tiled=True)


def across_line(value, axis, by):
    return lax.ppermute(value, axis, [(i, i ^ by) for i in range(4)])


def line(value, axis):
    return [value] + [across_line(value, axis, k) for k in range(1, 4)]


def after(gate, values):
    return lax.optimization_barrier((gate, values))


def relay(slabs, axis):
    near = [across_line(slabs[k], axis, k) for k in (1, 3)]
    near, far = after(near, slabs[2])
    return [slabs[0], near[0], across_line(far, axis, 2), near[1]]


def relay_far(slabs, axis):
    far, near = after(across_line(slabs[2], axis, 2), (slabs[1], slabs[3]))
    return [slabs[0], across_line(near[0], axis, 1), far, across_line(near[1], axis, 3)]


def swapped(joined):
    return joined, lax.ppermute(joined, "c", [(0, 1), (1, 0)])


def body(entering, norm_gain, query_weight, key_matrix, value_matrix, output_weight):
    plane, across, along, core = (lax.axis_index(name) for name in ALL)
    slot = 2 * core + lax.rem(along, 2)
    scalars = jnp.stack([plane, along, core]).astype(jnp.int32)

    inward = lambda layer: slab_in(layer, scalars, query_weight, key_matrix, value_matrix)

    rounds = []
    for r in range(4):
        pairs = []
        for p in range(4):
            for t in range(32):
                s = (t // 8 - r) % 4
                pairs.append((32 * p + t, 32 * p + 2 * ((2 * t) % 16 + s % 2) + s // 2))
        s = lax.rem(across - r + 4, 4)
        piece = lax.dynamic_slice(entering, (s // 2, 0, lax.rem(s, 2) * COLS), (1, SEQ, COLS))[0]
        gain = lax.dynamic_slice(norm_gain, (0, lax.rem(s, 2) * COLS), (1, COLS))
        piece = jnp.concatenate([piece, jnp.broadcast_to(gain, (8, COLS))], axis=0)
        rounds.append(lax.ppermute(piece, ALL, pairs))
    slab, cut = inward(0), slab_out(0, scalars, output_weight)
    near = [across_line(slab[k], "z", k) for k in (1, 3)]
    rounds, (near, far, cut) = after(rounds, (near, slab[2], cut))
    ins = [slab[0], near[0], across_line(far, "z", 2), near[1]]
    near = [across_line(cut[k], "y", k) for k in (1, 3)]
    rounds = jnp.stack(rounds)
    xs = [
        lax.dynamic_index_in_dim(
            rounds, lax.rem(lax.bitwise_xor(plane, k) - slot + 4, 4), 0, keepdims=False
        )[:SEQ]
        for k in range(4)
    ]
    gains = jnp.stack(
        [
            lax.dynamic_index_in_dim(rounds[:, SEQ], lax.rem(p - slot + 4, 4), 0, keepdims=False)
            for p in range(4)
        ]
    )
    ahead = inward(1)
    ins, (near, far, ahead, xs, gains) = after(ins, (near, cut[2], ahead, xs, gains))
    outs = [cut[0], near[0], across_line(far, "y", 2), near[1]]
    ins = swapped(join(ins))
    gains = jnp.stack(line(gains, "z")).astype(f32)
    states = []
    for layer in range(4):
        if layer:
            xs, outs = after(xs, outs)
        if layer < 3:
            xs, slab = after(xs, ahead)
            ins_next = relay_far(slab, "z")
        if layer:
            partial, outs = project(layer, scalars, xs, gains, ins, outs)
        else:
            partial = project(layer, scalars, xs, gains, ins, [])[0]
            partial, outs = after(partial, outs)
            outs = join(outs)
        if layer < 3:
            ins = ins_next
            partial, scalars = after(partial, scalars)
            cut = slab_out(layer + 1, scalars, output_weight)
            if layer < 2:
                ahead = inward(layer + 2)
        received, outs = after(exchange(partial, ("x", "y")), swapped(outs))
        if layer < 3:
            received, (cut, ahead) = after(received, (cut, ahead))
        mixed = line(attend(received), "y")
        if layer < 3:
            mixed, (ins, cut) = after(mixed, (ins, cut))
            outs_next = relay(cut, "y")
            partial, ins = output(scalars, mixed, outs, ins)
            ins = swapped(ins)
            outs = outs_next
        else:
            partial = output(scalars, mixed, outs, [])[0]
        x = close(exchange(partial, ("z", "x")), xs[0])
        states.append(x)
        if layer < 3:
            xs = line(x, "z")

    states = jnp.stack(states)
    rounds = []
    for k in range(4):
        pairs = [
            (2 * i + c, 32 * ((2 * c + i % 2 + k) % 4) + i // 2) for i in range(64) for c in range(2)
        ]
        piece = lax.dynamic_index_in_dim(states, lax.rem(slot + k, 4), 0, keepdims=False)
        rounds.append(lax.ppermute(piece, ALL, pairs))
    rounds = jnp.stack(rounds)
    pieces = [
        lax.dynamic_index_in_dim(rounds, lax.rem(plane - s + 4, 4), 0, keepdims=False) for s in range(4)
    ]
    return jnp.stack(
        [jnp.concatenate(pieces[:2], axis=1), jnp.concatenate(pieces[2:], axis=1)]
    )[None]


def solution(mesh):
    fine = Mesh(mesh.devices.reshape(4, 4, 4, 2), ALL)
    tp = ("x", "y", "c")
    rows = P(None, ALL, None)
    return jax.shard_map(
        body,
        mesh=fine,
        in_specs=(P(None, None, tp), P("z", tp), rows, rows, rows, rows),
        out_specs=P("z", None, None, tp),
        check_vma=False,
    )
```

```python
import functools
import math

import jax
import jax.numpy as jnp
from jax import lax
from jax.experimental import pallas as pl
from jax.experimental.pallas import tpu as pltpu
from jax.sharding import Mesh, PartitionSpec as P


ALL = ("z", "x", "y", "c")
HEAD = 128
SEQ = 88
COLS = 256
WIDTH = 16384
SLAB = 2304
OCOLS = 4096
ROWS = 272
VMEM_LIMIT = 52 * 1024 * 1024
f32 = jnp.float32
bf16 = jnp.bfloat16
SMEM = pl.BlockSpec(memory_space=pltpu.SMEM)
PARAMS = pltpu.CompilerParams(vmem_limit_bytes=VMEM_LIMIT)


def dot(a, b, contract=((1,), (0,))):
    return lax.dot_general(a, b, (contract, ((), ())), preferred_element_type=f32)


def whole(*shape):
    return pl.BlockSpec(shape, lambda s: (0,) * len(shape))


def cost(flops, size):
    return pl.CostEstimate(flops=flops, bytes_accessed=size, transcendentals=0)


def masks():
    rows = lax.broadcasted_iota(jnp.int32, (SEQ, 128), 0)
    lanes = lax.broadcasted_iota(jnp.int32, (SEQ, 128), 1)
    return rows == lanes, lanes <= rows


def slab_in_kernel(scalars, q_ref, k_ref, v_ref, *outs):
    for k, out in enumerate(outs):
        at = lax.bitwise_xor(scalars[0], k)
        out[:, :2048] = q_ref[0, :, pl.ds(pl.multiple_of(at * 2048, 2048), 2048)]
        out[:, 2048:2176] = k_ref[0, :, pl.ds(pl.multiple_of(at * 128, 128), 128)]
        out[:, 2176:] = v_ref[0, :, pl.ds(pl.multiple_of(at * 128, 128), 128)]


def slab_in(layer, scalars, q, k, v):
    return pl.pallas_call(
        slab_in_kernel,
        grid=(2,),
        in_specs=[
            SMEM,
            pl.BlockSpec((1, 64, 8192), lambda s: (layer, s, 0)),
            pl.BlockSpec((1, 64, 512), lambda s: (layer, s, 0)),
            pl.BlockSpec((1, 64, 512), lambda s: (layer, s, 0)),
        ],
        out_specs=[pl.BlockSpec((64, SLAB), lambda s: (s, 0))] * 4,
        out_shape=[pltpu.HBM((128, SLAB), bf16)] * 4,
        compiler_params=PARAMS if layer else pltpu.CompilerParams(vmem_limit_bytes=62 * 1024 * 1024),
        cost_estimate=cost(0, 4_700_000),
        name="slab_in",
    )(scalars, q, k, v)


def slab_out_kernel(scalars, o_ref, *outs):
    for k, out in enumerate(outs):
        at = lax.bitwise_xor(scalars[1], k) * COLS
        for s in range(16):
            out[:, COLS * s : COLS * s + COLS] = o_ref[
                0, :, pl.ds(pl.multiple_of(at + 1024 * s, COLS), COLS)
            ]


def slab_out(layer, scalars, o):
    return pl.pallas_call(
        slab_out_kernel,
        grid=(2,),
        in_specs=[SMEM, pl.BlockSpec((1, 32, WIDTH), lambda s: (layer, s, 0))],
        out_specs=[pl.BlockSpec((32, OCOLS), lambda s: (s, 0))] * 4,
        out_shape=[pltpu.HBM((64, OCOLS), bf16)] * 4,
        compiler_params=PARAMS,
        cost_estimate=cost(0, 4_200_000),
        name="slab_out",
    )(scalars, o)


def join_kernel(*refs):
    for k, ref in enumerate(refs[:4]):
        refs[4][k] = ref[...]


def join(pieces):
    rows, columns = pieces[0].shape
    half = rows // 2
    return pl.pallas_call(
        join_kernel,
        grid=(2,),
        in_specs=[pl.BlockSpec((half, columns), lambda s: (s, 0))] * 4,
        out_specs=pl.BlockSpec((4, half, columns), lambda s: (0, s, 0)),
        out_shape=pltpu.HBM((4, rows, columns), bf16),
        compiler_params=PARAMS,
        cost_estimate=cost(0, 4_500_000),
        name="join",
    )(*pieces)


def project_kernel(layer, scalars, *refs):
    xs, (gain_ref, own, other, kv_own, kv_other), refs = refs[:4], refs[4:9], refs[9:]
    if len(refs) == 8:
        pieces, out_ref, joined_ref = refs[:4], refs[4], refs[5]
        for k in range(4):
            joined_ref[k] = pieces[k][...]
    else:
        out_ref = refs[0]
    xg_ref, lead_ref = refs[-2:]
    z, core = scalars[0], scalars[2]

    @pl.when(pl.program_id(0) == 0)
    def _():
        rows = lax.broadcasted_iota(jnp.int32, (4, COLS), 0)
        gains = gain_ref[lax.bitwise_xor(z, layer)]
        total = jnp.zeros((SEQ, 1), f32)
        low, high = [], []
        for k in range(4):
            wide = xs[k][...].astype(f32)
            total += jnp.sum(wide * wide, axis=1, keepdims=True)
            at = rows == lax.bitwise_xor(z, k)
            scaled = wide * jnp.sum(jnp.where(at, gains, 0.0), axis=0, keepdims=True)
            low.append(scaled[:, :128])
            high.append(scaled[:, 128:])
        xg_ref[...] = jnp.where(
            core == 1, jnp.concatenate(high + low, axis=1), jnp.concatenate(low + high, axis=1)
        ).astype(bf16)
        eye, _ = masks()
        row = jnp.sum(jnp.where(eye, total, 0.0), axis=0, keepdims=True)
        coarse = row.astype(bf16).astype(f32)
        which = lax.broadcasted_iota(jnp.int32, (8, 128), 0)
        lead_ref[:8] = jnp.where(which == 0, coarse, jnp.where(which == 1, row - coarse, 0.0))
        kv = dot(xg_ref[:, :512], kv_own[...].reshape(512, 256))
        kv += dot(xg_ref[:, 512:], kv_other[...].reshape(512, 256))
        lead_ref[8 : 8 + SEQ] = kv[:, :128]
        lead_ref[8 + SEQ :] = kv[:, 128:]

    q = dot(xg_ref[:, :512], own[...].reshape(512, 1024))
    q += dot(xg_ref[:, 512:], other[...].reshape(512, 1024))
    for h in range(8):
        out_ref[h] = jnp.concatenate(
            [lead_ref[...], q[:, HEAD * h : HEAD * h + HEAD]], axis=0
        ).astype(bf16)


def project(layer, scalars, xs, gains, weights, pieces):
    specs = [SMEM] + [whole(SEQ, COLS)] * 4 + [whole(4, 4, COLS)]
    specs += [pl.BlockSpec((4, 128, 1024), lambda s: (0, 0, s))] * 2
    specs += [pl.BlockSpec((4, 128, 256), lambda s: (0, 0, 8))] * 2
    outs = [pltpu.HBM((16, ROWS, 128), bf16)]
    out_specs = [pl.BlockSpec((8, ROWS, 128), lambda s: (s, 0, 0))]
    if pieces:
        specs += [pl.BlockSpec((64, 2048), lambda s: (0, s))] * 4
        outs.append(pltpu.HBM((4, 64, OCOLS), bf16))
        out_specs.append(pl.BlockSpec((4, 64, 2048), lambda s: (0, 0, s)))
    return pl.pallas_call(
        functools.partial(project_kernel, layer),
        grid=(2,),
        in_specs=specs,
        out_specs=out_specs,
        out_shape=outs,
        scratch_shapes=[pltpu.VMEM((SEQ, 1024), bf16), pltpu.VMEM((8 + 2 * SEQ, 128), f32)],
        compiler_params=PARAMS,
        cost_estimate=cost(2 * SEQ * 1024 * SLAB, 10_000_000),
        name="project",
    )(scalars, *xs, gains, *weights, *weights, *pieces)


def attend_kernel(recv_ref, out_ref, acc):
    step = pl.program_id(0)

    @pl.when(step == 0)
    def _():
        acc[...] = jnp.sum(recv_ref[...].astype(f32), axis=0)

    @pl.when(step > 0)
    def _():
        acc[...] += jnp.sum(recv_ref[...].astype(f32), axis=0)

    @pl.when(step == 3)
    def _():
        row = lax.rsqrt((acc[0:1] + acc[1:2]) * (1.0 / WIDTH) + 1e-05)
        eye, _ = masks()
        column = jnp.sum(jnp.where(eye, row, 0.0), axis=1, keepdims=True)
        keys, values, queries = (
            (acc[8 + SEQ * k : 8 + SEQ * k + SEQ] * column).astype(bf16) for k in range(3)
        )
        scores = dot(queries, keys, ((1,), (1,))) * (1.0 / math.sqrt(HEAD))
        causal = lax.broadcasted_iota(jnp.int32, (SEQ, SEQ), 0) >= lax.broadcasted_iota(
            jnp.int32, (SEQ, SEQ), 1
        )
        weights = jnp.where(causal, jnp.exp(scores), 0.0)
        shares = (weights / jnp.sum(weights, axis=1, keepdims=True)).astype(bf16)
        out_ref[...] = dot(shares, values).astype(bf16)


def attend(received):
    return pl.pallas_call(
        attend_kernel,
        grid=(4,),
        in_specs=[pl.BlockSpec((4, ROWS, 128), lambda s: (s, 0, 0))],
        out_specs=whole(SEQ, HEAD),
        out_shape=jax.ShapeDtypeStruct((SEQ, HEAD), bf16),
        scratch_shapes=[pltpu.VMEM((ROWS, 128), f32)],
        compiler_params=PARAMS,
        cost_estimate=cost(6_000_000, 1_200_000),
        name="attend",
    )(received)


def output_kernel(scalars, *refs):
    mixed, own, other, mixed_ref = refs[:4], refs[4], refs[5], refs[-1]
    if len(refs) == 8:
        out_ref = refs[6]
    else:
        pieces, out_ref, joined_ref = refs[6:10], refs[10], refs[11]
        for k in range(4):
            joined_ref[k] = pieces[k][...]

    @pl.when(pl.program_id(0) == 0)
    def _():
        parts = [part[...].astype(f32) for part in mixed]
        low, high = [part[:, :64] for part in parts], [part[:, 64:] for part in parts]
        mixed_ref[...] = jnp.where(
            scalars[2] == 1, jnp.concatenate(high + low, axis=1), jnp.concatenate(low + high, axis=1)
        ).astype(bf16)

    o = dot(mixed_ref[:, :256], own[...].reshape(256, 2048))
    o += dot(mixed_ref[:, 256:], other[...].reshape(256, 2048))
    for i in range(8):
        out_ref[i] = o[:, COLS * i : COLS * i + COLS].astype(bf16)


def output(scalars, mixed, weights, pieces):
    specs = [SMEM] + [whole(SEQ, HEAD)] * 4 + [pl.BlockSpec((4, 64, 2048), lambda s: (0, 0, s))] * 2
    outs = [pltpu.HBM((16, SEQ, COLS), bf16)]
    out_specs = [pl.BlockSpec((8, SEQ, COLS), lambda s: (s, 0, 0))]
    if pieces:
        specs += [pl.BlockSpec((64, SLAB), lambda s: (s, 0))] * 4
        outs.append(pltpu.HBM((4, 128, SLAB), bf16))
        out_specs.append(pl.BlockSpec((4, 64, SLAB), lambda s: (0, s, 0)))
    return pl.pallas_call(
        output_kernel,
        grid=(2,),
        in_specs=specs,
        out_specs=out_specs,
        out_shape=outs,
        scratch_shapes=[pltpu.VMEM((SEQ, 512), bf16)],
        compiler_params=PARAMS,
        cost_estimate=cost(2 * SEQ * 512 * OCOLS, 10_000_000),
        name="output",
    )(scalars, *mixed, *weights, *pieces)


def close_kernel(recv_ref, x_ref, out_ref):
    out_ref[...] = (x_ref[...].astype(f32) + jnp.sum(recv_ref[...].astype(f32), axis=0)).astype(bf16)


def close(received, x):
    return pl.pallas_call(
        close_kernel,
        grid=(1,),
        in_specs=[whole(16, SEQ, COLS), whole(SEQ, COLS)],
        out_specs=whole(SEQ, COLS),
        out_shape=jax.ShapeDtypeStruct((SEQ, COLS), bf16),
        compiler_params=PARAMS,
        cost_estimate=cost(400_000, 800_000),
        name="close",
    )(received, x)


def exchange(value, axes):
    return lax.all_to_all(value, axes, 0, 0, tiled=True)


def across_line(value, axis, by):
    return lax.ppermute(value, axis, [(i, i ^ by) for i in range(4)])


def line(value, axis):
    return [value] + [across_line(value, axis, k) for k in range(1, 4)]


def after(gate, values):
    return lax.optimization_barrier((gate, values))


def relay(slabs, axis):
    near = [across_line(slabs[k], axis, k) for k in (1, 3)]
    near, far = after(near, slabs[2])
    return [slabs[0], near[0], across_line(far, axis, 2), near[1]]


def swapped(joined):
    return joined, lax.ppermute(joined, "c", [(0, 1), (1, 0)])


def body(entering, norm_gain, query_weight, key_matrix, value_matrix, output_weight):
    plane, across, along, core = (lax.axis_index(name) for name in ALL)
    slot = 2 * core + lax.rem(along, 2)
    scalars = jnp.stack([plane, along, core]).astype(jnp.int32)

    inward = lambda layer: slab_in(layer, scalars, query_weight, key_matrix, value_matrix)

    rounds = []
    for r in range(4):
        pairs = []
        for p in range(4):
            for t in range(32):
                s = (t // 8 - r) % 4
                pairs.append((32 * p + t, 32 * p + 2 * ((2 * t) % 16 + s % 2) + s // 2))
        s = lax.rem(across - r + 4, 4)
        piece = lax.dynamic_slice(entering, (s // 2, 0, lax.rem(s, 2) * COLS), (1, SEQ, COLS))[0]
        gain = lax.dynamic_slice(norm_gain, (0, lax.rem(s, 2) * COLS), (1, COLS))
        piece = jnp.concatenate([piece, jnp.broadcast_to(gain, (8, COLS))], axis=0)
        rounds.append(lax.ppermute(piece, ALL, pairs))
    slab, cut = inward(0), slab_out(0, scalars, output_weight)
    near = [across_line(slab[k], "z", k) for k in (1, 3)]
    rounds, (near, far, cut) = after(rounds, (near, slab[2], cut))
    ins = [slab[0], near[0], across_line(far, "z", 2), near[1]]
    near = [across_line(cut[k], "y", k) for k in (1, 3)]
    rounds = jnp.stack(rounds)
    xs = [
        lax.dynamic_index_in_dim(
            rounds, lax.rem(lax.bitwise_xor(plane, k) - slot + 4, 4), 0, keepdims=False
        )[:SEQ]
        for k in range(4)
    ]
    gains = jnp.stack(
        [
            lax.dynamic_index_in_dim(rounds[:, SEQ], lax.rem(p - slot + 4, 4), 0, keepdims=False)
            for p in range(4)
        ]
    )
    ahead = inward(1)
    ins, (near, far, ahead, xs, gains) = after(ins, (near, cut[2], ahead, xs, gains))
    outs = [cut[0], near[0], across_line(far, "y", 2), near[1]]
    ins = swapped(join(ins))
    gains = jnp.stack(line(gains, "z")).astype(f32)
    states = []
    for layer in range(4):
        if layer:
            xs, outs = after(xs, outs)
        if layer < 3:
            xs, slab = after(xs, ahead)
            ins_next = relay(slab, "z")
        if layer:
            partial, outs = project(layer, scalars, xs, gains, ins, outs)
        else:
            partial = project(layer, scalars, xs, gains, ins, [])[0]
            partial, outs = after(partial, outs)
            outs = join(outs)
        if layer < 3:
            ins = ins_next
            partial, scalars = after(partial, scalars)
            cut = slab_out(layer + 1, scalars, output_weight)
            if layer < 2:
                ahead = inward(layer + 2)
        received, outs = after(exchange(partial, ("x", "y")), swapped(outs))
        if layer < 3:
            received, (cut, ahead) = after(received, (cut, ahead))
        mixed = line(attend(received), "y")
        if layer < 3:
            mixed, cut = after(mixed, cut)
            outs_next = relay(cut, "y")
            partial = output(scalars, mixed, outs, [])[0]
            partial, ins = after(partial, ins)
            ins = swapped(join(ins))
            outs = outs_next
        else:
            partial = output(scalars, mixed, outs, [])[0]
        x = close(exchange(partial, ("z", "x")), xs[0])
        states.append(x)
        if layer < 3:
            xs = line(x, "z")

    states = jnp.stack(states)
    rounds = []
    for k in range(4):
        pairs = [
            (2 * i + c, 32 * ((2 * c + i % 2 + k) % 4) + i // 2) for i in range(64) for c in range(2)
        ]
        piece = lax.dynamic_index_in_dim(states, lax.rem(slot + k, 4), 0, keepdims=False)
        rounds.append(lax.ppermute(piece, ALL, pairs))
    rounds = jnp.stack(rounds)
    pieces = [
        lax.dynamic_index_in_dim(rounds, lax.rem(plane - s + 4, 4), 0, keepdims=False) for s in range(4)
    ]
    return jnp.stack(
        [jnp.concatenate(pieces[:2], axis=1), jnp.concatenate(pieces[2:], axis=1)]
    )[None]


def solution(mesh):
    fine = Mesh(mesh.devices.reshape(4, 4, 4, 2), ALL)
    tp = ("x", "y", "c")
    rows = P(None, ALL, None)
    return jax.shard_map(
        body,
        mesh=fine,
        in_specs=(P(None, None, tp), P("z", tp), rows, rows, rows, rows),
        out_specs=P("z", None, None, tp),
        check_vma=False,
    )
```
